256 devices in a mesh: gx: 8 (over z_hi, y), gy: 32 (over x, z_lo, core).
Axes of the slice: x: 4, y: 4, z: 8 (z_hi: 2, z_lo: 4; z = z_hi * 4 + z_lo), core: 2. Of those that a mesh axis runs over, the one named last changes fastest.
Arguments:
- disp: bfloat16 [40, 320, 26, 3], P('gx', 'gy'), may hold values from -6 to 6
- disp_prev: bfloat16 [40, 320, 26, 3], P('gx', 'gy'), may hold values from -6 to 6
- tangent: bfloat16 [40, 320, 4992], P('gx', 'gy'), may hold values from -6 to 6
- tangent_prev: bfloat16 [40, 320, 4992], P('gx', 'gy'), may hold values from -6 to 6
- lame_lambda: bfloat16 [8, 64, 5], P('gx', 'gy'), may hold values from 0.29882812 to 3
- lame_mu: bfloat16 [8, 64, 5], P('gx', 'gy'), may hold values from 0.29882812 to 3
- node_mass: float32 [40, 320, 26], P('gx', 'gy'), may hold values from 0.5 to 2
- force: bfloat16 [40, 320, 26, 3], P('gx', 'gy'), may hold values from -48 to 48
- cell_block: int32 [8, 64, 5], P('gx', 'gy'), may hold values from 0 to 63
- direction_block: int32 [64], replicated, may hold values from 0 to 63
- port_id: int32 [40, 320, 26], P('gx', 'gy'), may hold values from 0 to 64, as said below
- port_mode: bfloat16 [40, 320, 26, 3], P('gx', 'gy'), may hold values from -0.059814453 to 0.059814453
Outputs:
- disp_next: bfloat16 [40, 320, 26, 3], P('gx', 'gy')
- tangent_next: bfloat16 [40, 320, 4992], P('gx', 'gy')
- port_amp: float32 [64, 64], P('gy', 'gx')
The draws below stay inside these ranges and needn't reach their ends.
Inputs may be any that keep to these rules, and one draw needn't show every extreme that they name: `port_id`: 64 marks a node outside every output section; the output sections are the last 40 node layers along the second dimension, where every node belongs to some port; within each node line along the first dimension the port numbers never fall.
All inputs are finite; a program needn't handle non-finite values.
Results may differ from the reference program's by a relative error of at most 0.0016.
Values may be sent and summed in bfloat16 or wider, within the bound.
No kernel may reach another device: no remote copies, remote signals or barrier semaphores. Data moves between devices by JAX's collectives and lax.ppermute only.
A program may use at most 192 MiB of HBM per device.

```python
import math
import jax
import jax.numpy as jnp
import numpy as np
from jax import lax

EZ = 5
NT = 64
PORTS = 64
BLOCKS = 64
PORT_DEPTH = 40
EXG = 8
EYG = 64
NXN = 40
NYN = 320
NZN = 26


def draw_port_id(key, part):
    key = jax.random.fold_in(key, 11)
    shift_key = jax.random.fold_in(key, 1)
    phase_key = jax.random.fold_in(key, 2)
    reach = max(1, NXN // 4)
    edge_shift = jax.random.randint(shift_key, (1, NYN, NZN), -reach, reach + 1, dtype=jnp.int32)
    phase = jax.random.randint(phase_key, (1, NYN, NZN), 0, NXN, dtype=jnp.int32)
    layer_index = jnp.arange(NXN, dtype=jnp.int32)[:, None, None]
    banded = jnp.clip(((layer_index + edge_shift) * PORTS + phase) // NXN, 0, PORTS - 1)
    row_index = jnp.arange(NYN, dtype=jnp.int32)[None, :, None]
    return jnp.where(row_index >= NYN - PORT_DEPTH, banded, PORTS).astype(jnp.int32)


def touch_ends(entries, stream_key, smallest, largest):
    dims = entries.shape
    spot = [jax.random.randint(jax.random.fold_in(stream_key, axis), (), 0, dims[axis]) for axis in range(len(dims))]
    entries = entries.at[tuple(spot)].set(smallest)
    longest = dims.index(max(dims))
    spot[longest] = (spot[longest] + 1) % dims[longest]
    return entries.at[tuple(spot)].set(largest)


def block_levels(stream_key, dims, cuts, smallest, high):
    loudness, own = 1.0, jax.random.fold_in(stream_key, 6)
    for position, parts in cuts:
        steps = jnp.exp(jax.random.uniform(jax.random.fold_in(own, position), (parts,), jnp.float32, smallest / len(cuts), high / len(cuts)))
        loudness = loudness * jnp.repeat(steps, dims[position] // parts).reshape([-1 if axis == position else 1 for axis in range(len(dims))])
    return loudness


def gaussian(stream_key, shape, width, limit, split=(), kind=jnp.bfloat16):
    values = width * jax.random.normal(stream_key, shape, jnp.float32)
    if split:
        values = values * block_levels(stream_key, shape, split, -0.22, 0.18)
    return jnp.clip(values, -limit, limit).astype(kind)


def setup_inputs(seed: int = 0) -> dict:
    seeds = jax.random.split(jax.random.key(seed), 13)
    disp = gaussian(seeds[0], (NXN, NYN, NZN, 3), 1.0, 6.0, ((0, 8), (1, 32)))
    disp_prev = gaussian(seeds[1], (NXN, NYN, NZN, 3), 1.0, 6.0, ((0, 8), (1, 32)))
    tangent = gaussian(seeds[2], (NXN, NYN, NZN * 3 * NT), 1.0, 6.0, ((0, 8), (1, 32)))
    tangent_prev = gaussian(seeds[3], (NXN, NYN, NZN * 3 * NT), 1.0, 6.0, ((0, 8), (1, 32)))
    lame_lambda = jnp.clip(jnp.exp(math.log(3.0) - 2.306499 * jax.random.uniform(seeds[4], (EXG, EYG, EZ), jnp.float32) ** block_levels(seeds[4], (EXG, EYG, EZ), ((0, 8), (1, 32)), -0.2, 0.2)), 0.29882812, 3.0).astype(jnp.bfloat16)
    lame_mu = jnp.clip(jnp.exp(math.log(3.0) - 2.306499 * jax.random.uniform(seeds[5], (EXG, EYG, EZ), jnp.float32) ** block_levels(seeds[5], (EXG, EYG, EZ), ((0, 8), (1, 32)), -0.2, 0.2)), 0.29882812, 3.0).astype(jnp.bfloat16)
    node_mass = jnp.clip(jnp.exp(math.log(2.0) - 1.3862944 * jax.random.uniform(seeds[6], (NXN, NYN, NZN), jnp.float32) ** block_levels(seeds[6], (NXN, NYN, NZN), ((0, 8), (1, 32)), -0.2, 0.2)), 0.5, 2.0)
    force = gaussian(seeds[7], (NXN, NYN, NZN, 3), 8.0, 48.0, ((0, 8), (1, 32)))
    cell_block = touch_ends(jax.random.randint(seeds[8], (EXG, EYG, EZ), 0, BLOCKS), jax.random.fold_in(seeds[8], 1), 0, BLOCKS - 1).astype(jnp.int32)
    direction_block = touch_ends(jax.random.randint(seeds[9], (NT,), 0, BLOCKS), jax.random.fold_in(seeds[9], 1), 0, BLOCKS - 1).astype(jnp.int32)
    port_id = draw_port_id(jax.random.fold_in(seeds[12], 71), 0)
    port_mode = gaussian(seeds[11], (NXN, NYN, NZN, 3), 0.01, 0.059814453, ((0, 8), (1, 32)))
    return dict(disp=disp, disp_prev=disp_prev, tangent=tangent, tangent_prev=tangent_prev, lame_lambda=lame_lambda, lame_mu=lame_mu, node_mass=node_mass, force=force, cell_block=cell_block, direction_block=direction_block, port_id=port_id, port_mode=port_mode)


GLL_POINTS = np.array([-1.0, -0.765055323929465, -0.285231516480645, 0.285231516480645, 0.765055323929465, 1.0])
GLL_WEIGHTS = np.array([1.0 / 15.0, 0.378474956297847, 0.554858377035486, 0.554858377035486, 0.378474956297847, 1.0 / 15.0])
STEP_SQUARED = 0.03
HIGHEST = lax.Precision.HIGHEST
BACK_FORMS = ("pa,xpybzcn->xaybzcn", "pb,xaypzcn->xaybzcn", "pc,xaybzpn->xaybzcn")


def derivative_table():
    identity = np.eye(6)
    differences = GLL_POINTS[:, None] - GLL_POINTS[None, :] + identity
    barycentric = 1.0 / np.prod(differences, axis=1)
    matrix = (barycentric[None, :] / barycentric[:, None]) / differences
    matrix = matrix * (1.0 - identity)
    matrix = matrix - identity * matrix.sum(axis=1)[:, None]
    return matrix


def point_weights():
    cubed = GLL_WEIGHTS[:, None, None] * GLL_WEIGHTS[None, :, None] * GLL_WEIGHTS[None, None, :]
    return jnp.asarray(cubed.reshape(1, 6, 1, 6, 1, 6, 1), jnp.float32)


def split_axis(values, axis_at):
    values = jnp.moveaxis(values, axis_at, 0)
    elem_count = (values.shape[0] - 1) // 5
    main_part = values[:5 * elem_count].reshape((elem_count, 5) + values.shape[1:])
    tail_part = values[5::5][:, None]
    joined = jnp.concatenate([main_part, tail_part], axis=1)
    return jnp.moveaxis(joined, (0, 1), (axis_at, axis_at + 1))


def merge_axis(values, axis_at):
    values = jnp.moveaxis(values, (axis_at, axis_at + 1), (0, 1))
    elem_count = values.shape[0]
    rest_shape = values.shape[2:]
    main_part = values[:, :5].reshape((5 * elem_count,) + rest_shape)
    main_part = jnp.concatenate([main_part, jnp.zeros((1,) + rest_shape, values.dtype)], axis=0)
    tail_part = jnp.concatenate([values[:, 5:6], jnp.zeros((elem_count, 4) + rest_shape, values.dtype)], axis=1)
    tail_part = tail_part.reshape((5 * elem_count,) + rest_shape)
    tail_part = jnp.concatenate([jnp.zeros((5,) + rest_shape, values.dtype), tail_part], axis=0)[:5 * elem_count + 1]
    return jnp.moveaxis(main_part + tail_part, 0, axis_at)


def to_cells(values):
    return split_axis(split_axis(split_axis(values, 0), 2), 4)


def to_nodes(values):
    return merge_axis(merge_axis(merge_axis(values, 4), 2), 0)


def gradients(cells, deriv):
    return [
        jnp.einsum("pa,xaybzcn->xpybzcn", deriv, cells, precision=HIGHEST),
        jnp.einsum("pb,xaybzcn->xaypzcn", deriv, cells, precision=HIGHEST),
        jnp.einsum("pc,xaybzcn->xaybzpn", deriv, cells, precision=HIGHEST),
    ]


def internal_forces(gradient_list, lam_cells, mu_cells, deriv, weights, block_width):
    def column_block(values, component):
        return values[..., component * block_width:(component + 1) * block_width]

    dilation = column_block(gradient_list[0], 0) + column_block(gradient_list[1], 1) + column_block(gradient_list[2], 2)
    summed = None
    for direction in range(3):
        pieces = []
        for component in range(3):
            stress = mu_cells * (column_block(gradient_list[direction], component) + column_block(gradient_list[component], direction))
            if component == direction:
                stress = stress + lam_cells * dilation
            pieces.append(weights * stress)
        contribution = jnp.einsum(BACK_FORMS[direction], deriv, jnp.concatenate(pieces, axis=-1), precision=HIGHEST)
        summed = contribution if summed is None else summed + contribution
    return summed


def block_forces(primal_nodes, tangent_nodes, lam_cells, mu_cells, select):
    deriv = jnp.asarray(derivative_table(), jnp.float32)
    weights = point_weights()
    lam_wide = lam_cells.astype(jnp.float32)[:, None, :, None, :, None, None]
    mu_wide = mu_cells.astype(jnp.float32)[:, None, :, None, :, None, None]
    primal_grad = gradients(to_cells(primal_nodes).astype(jnp.float32), deriv)
    primal_force = internal_forces(primal_grad, lam_wide, mu_wide, deriv, weights, 1)
    sensitivity = internal_forces(primal_grad, 0.0, 1.0, deriv, weights, 1)
    tangent_grad = gradients(to_cells(tangent_nodes).astype(jnp.float32), deriv)
    directions = select.shape[-1]
    tangent_force = internal_forces(tangent_grad, lam_wide, mu_wide, deriv, weights, directions)
    source = sensitivity[..., :, None] * select.astype(jnp.float32)[:, None, :, None, :, None, None, :]
    tangent_force = tangent_force + source.reshape(tangent_force.shape)
    return to_nodes(primal_force), to_nodes(tangent_force)


def reference(disp, disp_prev, tangent, tangent_prev, lame_lambda, lame_mu, node_mass, force, cell_block, direction_block, port_id, port_mode):
    directions = direction_block.shape[0]
    node_shape = disp.shape[:3] + (3 * directions,)
    tangent = tangent.reshape(node_shape)
    tangent_prev = tangent_prev.reshape(node_shape)
    padding = ((0, 1), (0, 1), (0, 0), (0, 0))
    padded_disp = jnp.pad(disp, padding)
    padded_tangent = jnp.pad(tangent, padding)
    select = (cell_block[..., None] == direction_block[None, None, None, :]).astype(jnp.float32)

    def one_layer(layer_index, sums):
        primal_acc, tangent_acc = sums
        layer_at = jnp.asarray(layer_index).astype(jnp.int32)
        start = (layer_at * 5).astype(jnp.int32)
        node_disp = lax.dynamic_slice_in_dim(padded_disp, start, 6, 0)
        node_tangent = lax.dynamic_slice_in_dim(padded_tangent, start, 6, 0)
        lam_layer = lax.dynamic_slice_in_dim(lame_lambda, layer_at, 1, 0)
        mu_layer = lax.dynamic_slice_in_dim(lame_mu, layer_at, 1, 0)
        select_layer = lax.dynamic_slice_in_dim(select, layer_at, 1, 0)
        primal_part, tangent_part = block_forces(node_disp, node_tangent, lam_layer, mu_layer, select_layer)
        primal_acc = lax.dynamic_update_slice_in_dim(primal_acc, lax.dynamic_slice_in_dim(primal_acc, start, 6, 0) + primal_part, start, 0)
        tangent_acc = lax.dynamic_update_slice_in_dim(tangent_acc, lax.dynamic_slice_in_dim(tangent_acc, start, 6, 0) + tangent_part, start, 0)
        return primal_acc, tangent_acc

    initial = (jnp.zeros(padded_disp.shape, jnp.float32), jnp.zeros(padded_tangent.shape, jnp.float32))
    primal_acc, tangent_acc = lax.fori_loop(0, lame_lambda.shape[0], one_layer, initial)
    primal_force = primal_acc[:disp.shape[0], :disp.shape[1]]
    tangent_force = tangent_acc[:disp.shape[0], :disp.shape[1]]
    mass = node_mass[..., None]
    disp_next = (2.0 * disp.astype(jnp.float32) - disp_prev.astype(jnp.float32) + STEP_SQUARED * (force.astype(jnp.float32) - primal_force) / mass).astype(jnp.bfloat16)
    tangent_full = 2.0 * tangent.astype(jnp.float32) - tangent_prev.astype(jnp.float32) - STEP_SQUARED * tangent_force / mass
    modes = port_mode.astype(jnp.float32)
    weighted = modes[..., 0:1] * tangent_full[..., 0:directions]
    weighted = weighted + modes[..., 1:2] * tangent_full[..., directions:2 * directions]
    weighted = weighted + modes[..., 2:3] * tangent_full[..., 2 * directions:3 * directions]
    port_amp = jax.ops.segment_sum(weighted.reshape(-1, directions), port_id.reshape(-1), num_segments=PORTS + 1)[:PORTS]
    tangent_next = tangent_full.astype(jnp.bfloat16).reshape(disp.shape[0], disp.shape[1], -1)
    return disp_next, tangent_next, port_amp
```

```python
import functools

import jax
import jax.numpy as jnp
import ml_dtypes
import numpy as np
from jax import lax
from jax.experimental import pallas as pl
from jax.experimental.pallas import tpu as pltpu
from jax.sharding import PartitionSpec as P

PORTS = 64
GLL_POINTS = np.array(
    [-1.0, -0.765055323929465, -0.285231516480645, 0.285231516480645, 0.765055323929465, 1.0]
)
GLL_WEIGHTS = np.array(
    [
        1.0 / 15.0,
        0.378474956297847,
        0.554858377035486,
        0.554858377035486,
        0.378474956297847,
        1.0 / 15.0,
    ]
)
STEP_SQUARED = 0.03
HIGHEST = lax.Precision.HIGHEST
F32 = jnp.float32
BF16 = jnp.bfloat16

NX, NY, NZ = 5, 10, 26
COLS = 4992
SMALL = 384
WIDE = COLS + SMALL
BACK = COLS + 128
ROWS = 96
PTS = 72
VMEM_LIMIT = 48 * 1024 * 1024


def derivative_table():
    identity = np.eye(6)
    differences = GLL_POINTS[:, None] - GLL_POINTS[None, :] + identity
    barycentric = 1.0 / np.prod(differences, axis=1)
    matrix = barycentric[None, :] / barycentric[:, None] / differences
    matrix = matrix * (1.0 - identity)
    matrix = matrix - identity * matrix.sum(axis=1)[:, None]
    return matrix


def halves(matrix):
    matrix = matrix.astype(np.float32)
    high = matrix.astype(ml_dtypes.bfloat16)
    low = (matrix - high.astype(np.float32)).astype(ml_dtypes.bfloat16)
    return high, low


SYM = {(0, 0): 0, (1, 1): 1, (2, 2): 2, (0, 1): 3, (0, 2): 4, (1, 2): 5}


def sym_of(c, d):
    return SYM[(min(c, d), max(c, d))]


@functools.cache
def tables():
    deriv = derivative_table()
    w = GLL_WEIGHTS
    fx = np.zeros((PTS, ROWS))
    fy = np.zeros((PTS, ROWS))
    fv = np.zeros((PTS, ROWS))
    wxy = np.zeros(PTS)
    for e in range(2):
        for px in range(6):
            for py in range(6):
                r = e * 36 + px * 6 + py
                wxy[r] = w[px] * w[py]
                fv[r, 16 * px + 5 * e + py] = 1.0
                for a in range(6):
                    fx[r, 16 * a + 5 * e + py] += deriv[px, a]
                    fy[r, 16 * px + 5 * e + a] += deriv[py, a]
    forward = np.concatenate([fx, fy, fv], axis=0)
    f_high, f_low = halves(forward)
    forward2 = np.concatenate([f_high, f_low], axis=1)
    backward = np.concatenate([(m * wxy[:, None]).T for m in (fx, fy, fv)], axis=1)
    b_high, b_low = halves(backward)
    backward2 = np.concatenate([b_high, b_low], axis=0)

    coef = np.zeros((2, 39, 128))
    for n in range(3):
        for m in range(3):
            a = np.repeat([deriv[2 * n, 2 * m], deriv[2 * n + 1, 2 * m + 1]], 64)
            b = np.repeat([deriv[2 * n, 2 * m + 1], deriv[2 * n + 1, 2 * m]], 64)
            at = np.repeat([deriv[2 * m, 2 * n], deriv[2 * m + 1, 2 * n + 1]], 64)
            bt = np.repeat([deriv[2 * m + 1, 2 * n], deriv[2 * m, 2 * n + 1]], 64)
            for q, v in enumerate((a, b, at, bt)):
                coef[0, q * 9 + n * 3 + m] = v
                coef[1, q * 9 + n * 3 + m] = np.roll(v, 64)
    for m in range(3):
        v = np.repeat([w[2 * m], w[2 * m + 1]], 64)
        coef[0, 36 + m] = v
        coef[1, 36 + m] = np.roll(v, 64)
    coef = np.repeat(coef.reshape(78, 1, 128), 8, axis=1).astype(np.float32)

    to_sym = np.zeros((3, 128, 512))
    from_sym = np.zeros((256, 384))
    for i in range(5):
        for kp in range(6):
            base = i * 36 + kp * 6
            point_column = (5 * i + kp) * 3
            for c in range(3):
                for d in range(3):
                    s = base + sym_of(c, d)
                    share = 2.0 if c == d else 1.0
                    targets = [(s, share)]
                    if c == d:
                        targets += [(256 + base + q, 1.0) for q in range(3)]
                    for column, factor in targets:
                        if d < 2:
                            to_sym[d, point_column + c, column] += factor
                        else:
                            for k in range(6):
                                to_sym[2, (5 * i + k) * 3 + c, column] += factor * deriv[kp, k]
                    if d < 2:
                        from_sym[s, d * 128 + point_column + c] += w[kp]
                    else:
                        for k in range(6):
                            from_sym[s, 256 + (5 * i + k) * 3 + c] += w[kp] * deriv[kp, k]
    spread = np.zeros((128, 128))
    for piece in range(3):
        for k in range(NZ):
            for c in range(3):
                spread[piece * NZ + k, k * 3 + c] = 1.0
    return dict(
        forward=forward2,
        backward=backward2,
        back32=backward.astype(np.float32),
        coef=coef,
        to_sym=to_sym.reshape(384, 512).astype(np.float32),
        from_sym=from_sym.astype(np.float32),
        spread=spread.astype(ml_dtypes.bfloat16),
    )


def pack_kernel(t_ref, s_ref, x_ref, y_ref, c_ref, wide_ref):
    x_ref[:, :COLS] = t_ref[0]
    x_ref[:, COLS:] = s_ref[0]
    for x in range(NX):
        wide_ref[x : x + 1, :COLS] = t_ref[x, 0:1, :].astype(F32)
        wide_ref[x : x + 1, COLS:] = s_ref[x, 0:1, :].astype(F32)
    y_ref[...] = wide_ref[0:NX, :].astype(BF16)
    c_ref[...] = wide_ref[0:1, :].astype(BF16)


def fdot(a, b):
    return jnp.dot(a, b, preferred_element_type=F32, precision=HIGHEST)


def bdot(a, b):
    return jnp.dot(a, b, preferred_element_type=F32)


def split(value):
    high = value.astype(BF16)
    return high, (value - high.astype(F32)).astype(BF16)


def main_kernel(
    par_ref,
    cell_ref,
    t_ref,
    tp_ref,
    s_ref,
    loc_ref,
    hx_ref,
    hy_ref,
    hc_ref,
    lanes_ref,
    dirs_ref,
    fwd_ref,
    bwd_ref,
    back32_ref,
    coef_ref,
    to_sym_ref,
    from_sym_ref,
    spread_ref,
    part_ref,
    dpart_ref,
    rx_ref,
    ry_ref,
    rc_ref,
    amp_ref,
    wide,
    u2,
    grad,
    stress,
    force,
    sym,
    rowpar,
    edge,
):
    for x in range(NX):
        wide[16 * x + 8 : 16 * x + 16, :] = jnp.zeros((8, WIDE), F32)
        wide[16 * x : 16 * x + NY, :COLS] = t_ref[x].astype(F32)
        wide[16 * x : 16 * x + NY, COLS:] = s_ref[x].astype(F32)
        wide[16 * x + NY : 16 * x + NY + 1, :] = hy_ref[x : x + 1, :].astype(F32)
    wide[88:96, :] = jnp.zeros((8, WIDE), F32)
    wide[80 : 80 + NY, :] = hx_ref[...].astype(F32)
    wide[80 + NY : 81 + NY, :] = hc_ref[...].astype(F32)
    u2[0:ROWS, :] = wide[...].astype(BF16)
    u2[ROWS : 2 * ROWS, :] = u2[0:ROWS, :]

    fwd = fwd_ref[...]
    bwd = bwd_ref[...]
    low_half = lax.broadcasted_iota(jnp.int32, (8, 128), 1) < 64
    low_rows = lax.broadcasted_iota(jnp.int32, (ROWS, 128), 1) < 64
    first_el = lax.broadcasted_iota(jnp.int32, (PTS, 128), 0) < 36
    first_el2 = lax.broadcasted_iota(jnp.int32, (PTS, 256), 0) < 36

    pg = bdot(fwd, u2[:, COLS : COLS + 128])
    both = fdot(pg[0:PTS], to_sym_ref[0:128, :])
    both = both + fdot(pg[PTS : 2 * PTS], to_sym_ref[128:256, :])
    both = both + fdot(pg[2 * PTS : 3 * PTS], to_sym_ref[256:384, :])
    sym[...] = both[:, 0:256]
    lam_l = jnp.where(first_el2, lanes_ref[0:1, :], lanes_ref[1:2, :])
    mu_l = jnp.where(first_el2, lanes_ref[2:3, :], lanes_ref[3:4, :])
    primal_stress = lam_l * both[:, 256:512] + mu_l * both[:, 0:256]
    spread_out = fdot(primal_stress, from_sym_ref[...])
    primal_force = (
        fdot(back32_ref[:, 0:PTS], spread_out[:, 0:128])
        + fdot(back32_ref[:, PTS : 2 * PTS], spread_out[:, 128:256])
        + fdot(back32_ref[:, 2 * PTS : 3 * PTS], spread_out[:, 256:384])
    )

    force[...] = jnp.zeros((ROWS, COLS), F32)

    for i in range(5):
        odd = i % 2
        start = 960 * i - 64 * odd
        count = 9 + odd
        grad[:, 0 : count * 128] = bdot(fwd, u2[:, start : start + count * 128])
        rowpar[0] = jnp.where(first_el, par_ref[0, i], par_ref[0, 5 + i])
        rowpar[1] = jnp.where(first_el, par_ref[1, i], par_ref[1, 5 + i])
        cell = jnp.where(first_el, cell_ref[0, i], cell_ref[0, 5 + i])
        rowpar[2] = jnp.where(cell == dirs_ref[...], 1.0, 0.0)

        def rows_step(rc, carry, i=i, odd=odd):
            row = pl.multiple_of(rc * 8, 8)

            def tile(kind, index):
                at = pl.multiple_of(kind * PTS + rc * 8, 8)
                return grad[pl.ds(at, 8), index * 128 : (index + 1) * 128]

            def coef(index):
                return coef_ref[odd * 39 + index]

            values = []
            for kind in range(3):
                of_c = [[], [], []]
                for m in range(3):
                    if odd:
                        t0, t1, t2, t3 = (tile(kind, 3 * m + q) for q in range(4))
                        of_c[0].append(jnp.where(low_half, t2, t0))
                        of_c[1].append(pltpu.roll(jnp.where(low_half, t1, t2), 64, 1))
                        of_c[2].append(jnp.where(low_half, t3, t1))
                    else:
                        t0, t1, t2 = (tile(kind, 3 * m + q) for q in range(3))
                        of_c[0].append(jnp.where(low_half, t0, t1))
                        of_c[1].append(pltpu.roll(jnp.where(low_half, t2, t0), 64, 1))
                        of_c[2].append(jnp.where(low_half, t1, t2))
                values.append(of_c)
            gz = []
            for c in range(3):
                turned = [pltpu.roll(v, 64, 1) for v in values[2][c]]
                gz.append(
                    [
                        sum(
                            coef(n * 3 + m) * values[2][c][m] + coef(9 + n * 3 + m) * turned[m]
                            for m in range(3)
                        )
                        for n in range(3)
                    ]
                )
            g = [values[0], values[1], gz]
            lam = rowpar[0, pl.ds(row, 8), :]
            mu = rowpar[1, pl.ds(row, 8), :]
            sel = rowpar[2, pl.ds(row, 8), :]
            sym_rows = sym[pl.ds(row, 8), :]
            z_stress = [[None] * 3 for _ in range(3)]

            def put(direction, c, m, value):
                at = pl.multiple_of(direction * PTS + rc * 8, 8)
                stress[pl.ds(at, 8), (c * 3 + m) * 128 : (c * 3 + m + 1) * 128] = value

            for m in range(3):
                wz = coef(36 + m)
                muw = mu * wz
                lamw = lam * wz
                selw = sel * wz
                dil = lamw * (g[0][0][m] + g[1][1][m] + g[2][2][m])
                for c in range(3):
                    for d in range(c, 3):
                        s = i * 36 + sym_of(c, d)
                        first, second = s + (2 * m + odd) * 6, s + (2 * m + 1 - odd) * 6
                        src = jnp.where(
                            low_half,
                            jnp.broadcast_to(sym_rows[:, first : first + 1], (8, 128)),
                            jnp.broadcast_to(sym_rows[:, second : second + 1], (8, 128)),
                        )
                        value = muw * (g[d][c][m] + g[c][d][m]) + selw * src
                        if c == d:
                            value = value + dil
                        for a, b in [(c, d)] if c == d else [(c, d), (d, c)]:
                            if b == 2:
                                z_stress[a][m] = value
                            else:
                                put(b, a, m, value)
            for c in range(3):
                turned = [pltpu.roll(v, 64, 1) for v in z_stress[c]]
                for n in range(3):
                    value = sum(
                        coef(18 + n * 3 + m) * z_stress[c][m] + coef(27 + n * 3 + m) * turned[m]
                        for m in range(3)
                    )
                    put(2, c, n, value)
            return carry

        lax.fori_loop(0, 9, rows_step, 0)
        s_high, s_low = split(stress[...])
        two = bdot(bwd, s_high)
        nodes = two[0:ROWS] + two[ROWS : 2 * ROWS] + bdot(bwd[0:ROWS], s_low)

        def node_tile(c, m, nodes=nodes):
            return nodes[:, (c * 3 + m) * 128 : (c * 3 + m + 1) * 128]

        tile0 = start // 128

        def add(index, value, tile0=tile0):
            at = (tile0 + index) * 128
            force[:, at : at + 128] = force[:, at : at + 128] + value

        zero = jnp.zeros((ROWS, 128), F32)
        last_c2 = zero
        for m in range(3):
            c0, c2 = node_tile(0, m), node_tile(2, m)
            c1 = pltpu.roll(node_tile(1, m), 64, 1)
            if odd:
                add(3 * m, jnp.where(low_rows, last_c2, c0))
                add(3 * m + 1, jnp.where(low_rows, c1, c2))
                add(3 * m + 2, jnp.where(low_rows, c0, c1))
                last_c2 = c2
            else:
                add(3 * m, jnp.where(low_rows, c0, c1))
                add(3 * m + 1, jnp.where(low_rows, c2, c0))
                add(3 * m + 2, jnp.where(low_rows, c1, c2))
        if odd:
            add(9, jnp.where(low_rows, last_c2, zero))

    mass = bdot(u2[0:ROWS, COLS + 256 : COLS + 384], spread_ref[...])
    rate = STEP_SQUARED / jnp.where(mass > 0.0, mass, 1.0)
    primal_step = -rate * primal_force
    for x in range(NX):
        now = wide[16 * x : 16 * x + NY, COLS : COLS + 128]
        dpart_ref[x] = (
            primal_step[16 * x : 16 * x + NY, :]
            + 2.0 * now
            - loc_ref[x].astype(F32)
            + rate[16 * x : 16 * x + NY, :] * loc_ref[NX + x].astype(F32)
        )
    edge[:, COLS:BACK] = jnp.zeros((8, 128), F32)
    rx_ref[:, COLS:] = primal_step[80 : 80 + NY, :].astype(BF16)
    for x in range(NX):
        edge[x : x + 1, COLS:BACK] = primal_step[16 * x + NY : 16 * x + NY + 1, :]
    rc_ref[:, COLS:] = primal_step[80 + NY : 81 + NY, :].astype(BF16)

    ids = jnp.transpose(wide[:, COLS : COLS + 128])
    modes = jnp.transpose(wide[:, COLS + 128 : COLS + 256])
    port = lax.broadcasted_iota(jnp.int32, (PORTS, ROWS), 0).astype(F32)
    total = jnp.zeros((128, 128), F32)
    for tile in range(39):
        k0, k1 = (2 * tile) // 3, (2 * tile + 1) // 3
        at = slice(tile * 128, (tile + 1) * 128)
        r0 = jnp.broadcast_to(rate[:, 3 * k0 : 3 * k0 + 1], (ROWS, 128))
        if k1 != k0:
            r1 = jnp.broadcast_to(rate[:, 3 * k1 : 3 * k1 + 1], (ROWS, 128))
            r0 = jnp.where(low_rows, r0, r1)
        force[:, at] = -r0 * force[:, at]
        for x in range(NX):
            rows = slice(16 * x, 16 * x + NY)
            now = force[rows, at] + 2.0 * wide[rows, at] - tp_ref[x, :, at].astype(F32)
            force[rows, at] = now
            part_ref[x, :, at] = now
        high, low = split(force[:, at])
        picked = []
        for h, k in ((2 * tile, k0), (2 * tile + 1, k1)):
            same = ids[78 + k : 79 + k, :] == port
            picked.append(jnp.where(same, modes[h : h + 1, :], 0.0))
        left = jnp.concatenate(picked, axis=0).astype(BF16)
        total = total + bdot(left, high) + bdot(left, low)
    rx_ref[:, :COLS] = force[80 : 80 + NY, :].astype(BF16)
    for x in range(NX):
        edge[x : x + 1, :COLS] = force[16 * x + NY : 16 * x + NY + 1, :]
    ry_ref[...] = edge[0:NX, :].astype(BF16)
    rc_ref[:, :COLS] = force[80 + NY : 81 + NY, :].astype(BF16)
    amp_ref[...] = total[0:64, 0:64] + pltpu.roll(total[64:128, :], 64, 1)[:, 0:64]


def last_kernel(part_ref, dpart_ref, rx_ref, ry_ref, rc_ref, t_ref, d_ref):
    first = lax.broadcasted_iota(jnp.int32, (NY, COLS), 0) == 0
    first_d = lax.broadcasted_iota(jnp.int32, (NY, 128), 0) == 0
    for x in range(NX):
        row = ry_ref[x : x + 1, :].astype(F32)
        if x == 0:
            row = row + rc_ref[...].astype(F32)
        value = part_ref[x] + jnp.where(first, row[:, :COLS], 0.0)
        dvalue = dpart_ref[x] + jnp.where(first_d, row[:, COLS:], 0.0)
        if x == 0:
            value = value + rx_ref[:, :COLS].astype(F32)
            dvalue = dvalue + rx_ref[:, COLS:].astype(F32)
        t_ref[x] = value.astype(BF16)
        d_ref[x] = dvalue[:, :78].astype(BF16)


def per_device(
    disp,
    disp_prev,
    tangent,
    tangent_prev,
    lame_lambda,
    lame_mu,
    node_mass,
    force,
    cell_block,
    direction_block,
    port_id,
    port_mode,
):
    tab = tables()
    nx_dev, ny_dev = lax.axis_size("gx"), lax.axis_size("gy")
    vmem = pl.BlockSpec(memory_space=pltpu.VMEM)
    smem = pl.BlockSpec(memory_space=pltpu.SMEM)
    params = pltpu.CompilerParams(vmem_limit_bytes=VMEM_LIMIT)

    def step(shift_x, shift_y):
        route = []
        for i in range(nx_dev):
            for j in range(ny_dev):
                a, b = i + shift_x, j + shift_y
                if 0 <= a < nx_dev and 0 <= b < ny_dev:
                    route.append((i * ny_dev + j, a * ny_dev + b))
        return route

    def send(block, shift_x, shift_y):
        return lax.ppermute(block, ("gx", "gy"), step(shift_x, shift_y))

    flat = jnp.concatenate([disp, port_mode, disp_prev, force], axis=0).reshape(20, NY, 78)
    flat = jnp.pad(flat, ((0, 0), (0, 0), (0, 50)))
    m1 = lax.reduce_precision(node_mass, 8, 7)
    m2 = lax.reduce_precision(node_mass - m1, 8, 7)
    m3 = node_mass - m1 - m2
    gap = jnp.zeros((NX, NY, 50), BF16)
    small = jnp.concatenate(
        [
            flat[0:5, :, 0:78],
            port_id.astype(BF16),
            gap[:, :, 0:24],
            flat[5:10],
            m1.astype(BF16),
            m2.astype(BF16),
            m3.astype(BF16),
            gap,
        ],
        axis=-1,
    )
    local = flat[10:20]

    face_x, face_y, corner = pl.pallas_call(
        pack_kernel,
        out_shape=(
            jax.ShapeDtypeStruct((NY, WIDE), BF16),
            jax.ShapeDtypeStruct((NX, WIDE), BF16),
            jax.ShapeDtypeStruct((1, WIDE), BF16),
        ),
        in_specs=[vmem, vmem],
        out_specs=(vmem, vmem, vmem),
        scratch_shapes=[pltpu.VMEM((8, WIDE), F32)],
        compiler_params=params,
    )(tangent, small)
    halo_x = send(face_x, -1, 0)
    halo_y = send(face_y, 0, -1)
    halo_c = send(corner, -1, -1)

    par = jnp.stack([lame_lambda.reshape(10), lame_mu.reshape(10)]).astype(F32)
    cells = cell_block.reshape(1, 10)
    by_lane = jnp.repeat(par.reshape(4, 5), 36, axis=1)
    by_lane = jnp.pad(by_lane, ((0, 0), (0, 76)))
    dirs = jnp.concatenate([direction_block, direction_block]).reshape(1, 128)

    part, dpart, ret_x, ret_y, ret_c, amp = pl.pallas_call(
        main_kernel,
        out_shape=(
            jax.ShapeDtypeStruct((NX, NY, COLS), F32),
            jax.ShapeDtypeStruct((NX, NY, 128), F32),
            jax.ShapeDtypeStruct((NY, BACK), BF16),
            jax.ShapeDtypeStruct((NX, BACK), BF16),
            jax.ShapeDtypeStruct((1, BACK), BF16),
            jax.ShapeDtypeStruct((PORTS, 64), F32),
        ),
        in_specs=[smem, smem] + [vmem] * 16,
        out_specs=(vmem,) * 6,
        scratch_shapes=[
            pltpu.VMEM((ROWS, WIDE), F32),
            pltpu.VMEM((2 * ROWS, WIDE), BF16),
            pltpu.VMEM((3 * PTS, 1280), F32),
            pltpu.VMEM((3 * PTS, 1152), F32),
            pltpu.VMEM((ROWS, COLS), F32),
            pltpu.VMEM((PTS, 256), F32),
            pltpu.VMEM((3, PTS, 128), F32),
            pltpu.VMEM((8, BACK), F32),
        ],
        compiler_params=params,
    )(
        par,
        cells,
        tangent,
        tangent_prev,
        small,
        local,
        halo_x,
        halo_y,
        halo_c,
        by_lane,
        dirs,
        jnp.asarray(tab["forward"]),
        jnp.asarray(tab["backward"]),
        jnp.asarray(tab["back32"]),
        jnp.asarray(tab["coef"]),
        jnp.asarray(tab["to_sym"]),
        jnp.asarray(tab["from_sym"]),
        jnp.asarray(tab["spread"]),
    )

    back_x = send(ret_x, 1, 0)
    back_y = send(ret_y, 0, 1)
    back_c = send(ret_c, 1, 1)

    port_rows, port_cols = PORTS // ny_dev, 64 // nx_dev
    shares = amp.reshape(ny_dev, port_rows, nx_dev, port_cols).transpose(2, 0, 1, 3)
    shares = shares.reshape(nx_dev * ny_dev, port_rows * port_cols)
    shares = lax.all_to_all(shares, ("gx", "gy"), 0, 0)
    port_amp = shares.sum(axis=0).reshape(port_rows, port_cols)

    tangent_next, disp_next = pl.pallas_call(
        last_kernel,
        out_shape=(
            jax.ShapeDtypeStruct((NX, NY, COLS), BF16),
            jax.ShapeDtypeStruct((NX, NY, 78), BF16),
        ),
        in_specs=[vmem] * 5,
        out_specs=(vmem, vmem),
        compiler_params=params,
    )(part, dpart, back_x, back_y, back_c)
    return (disp_next.reshape(NX, NY, NZ, 3), tangent_next, port_amp)


def solution(mesh):
    return jax.shard_map(
        per_device,
        mesh=mesh,
        in_specs=(
            P("gx", "gy", None, None),
            P("gx", "gy", None, None),
            P("gx", "gy", None),
            P("gx", "gy", None),
            P("gx", "gy", None),
            P("gx", "gy", None),
            P("gx", "gy", None),
            P("gx", "gy", None, None),
            P("gx", "gy", None),
            P(),
            P("gx", "gy", None),
            P("gx", "gy", None, None),
        ),
        out_specs=(P("gx", "gy", None, None), P("gx", "gy", None), P("gy", "gx")),
        check_vma=False,
    )
```

```python
import functools

import jax
import jax.numpy as jnp
import ml_dtypes
import numpy as np
from jax import lax
from jax.experimental import pallas as pl
from jax.experimental.pallas import tpu as pltpu
from jax.sharding import PartitionSpec as P

PORTS = 64
GLL_POINTS = np.array(
    [-1.0, -0.765055323929465, -0.285231516480645, 0.285231516480645, 0.765055323929465, 1.0]
)
GLL_WEIGHTS = np.array(
    [
        1.0 / 15.0,
        0.378474956297847,
        0.554858377035486,
        0.554858377035486,
        0.378474956297847,
        1.0 / 15.0,
    ]
)
STEP_SQUARED = 0.03
HIGHEST = lax.Precision.HIGHEST
F32 = jnp.float32
BF16 = jnp.bfloat16

NX, NY, NZ = 5, 10, 26
COLS = 4992
SMALL = 384
WIDE = COLS + SMALL
BACK = COLS + 128
ROWS = 96
PTS = 72
VMEM_LIMIT = 24 * 1024 * 1024
VMEM_MOST = 60 * 1024 * 1024
UNROLL = 9
LONG_FLOPS = 4_000_000
LONG_BYTES = 8_000_000


def derivative_table():
    identity = np.eye(6)
    differences = GLL_POINTS[:, None] - GLL_POINTS[None, :] + identity
    barycentric = 1.0 / np.prod(differences, axis=1)
    matrix = barycentric[None, :] / barycentric[:, None] / differences
    matrix = matrix * (1.0 - identity)
    matrix = matrix - identity * matrix.sum(axis=1)[:, None]
    return matrix


def halves(matrix):
    matrix = matrix.astype(np.float32)
    high = matrix.astype(ml_dtypes.bfloat16)
    low = (matrix - high.astype(np.float32)).astype(ml_dtypes.bfloat16)
    return high, low


SYM = {(0, 0): 0, (1, 1): 1, (2, 2): 2, (0, 1): 3, (0, 2): 4, (1, 2): 5}


def sym_of(c, d):
    return SYM[(min(c, d), max(c, d))]


@functools.cache
def tables():
    deriv = derivative_table()
    w = GLL_WEIGHTS
    fx = np.zeros((PTS, ROWS))
    fy = np.zeros((PTS, ROWS))
    fv = np.zeros((PTS, ROWS))
    wxy = np.zeros(PTS)
    for e in range(2):
        for px in range(6):
            for py in range(6):
                r = e * 36 + px * 6 + py
                wxy[r] = w[px] * w[py]
                fv[r, 16 * px + 5 * e + py] = 1.0
                for a in range(6):
                    fx[r, 16 * a + 5 * e + py] += deriv[px, a]
                    fy[r, 16 * px + 5 * e + a] += deriv[py, a]
    forward = np.concatenate([fx, fy, fv], axis=0)
    f_high, f_low = halves(forward)
    forward2 = np.concatenate([f_high, f_low], axis=1)
    backward = np.concatenate([(m * wxy[:, None]).T for m in (fx, fy, fv)], axis=1)
    b_high, b_low = halves(backward)
    backward2 = np.concatenate([b_high, b_low], axis=0)

    coef = np.zeros((2, 39, 128))
    for n in range(3):
        for m in range(3):
            a = np.repeat([deriv[2 * n, 2 * m], deriv[2 * n + 1, 2 * m + 1]], 64)
            b = np.repeat([deriv[2 * n, 2 * m + 1], deriv[2 * n + 1, 2 * m]], 64)
            at = np.repeat([deriv[2 * m, 2 * n], deriv[2 * m + 1, 2 * n + 1]], 64)
            bt = np.repeat([deriv[2 * m + 1, 2 * n], deriv[2 * m, 2 * n + 1]], 64)
            for q, v in enumerate((a, b, at, bt)):
                coef[0, q * 9 + n * 3 + m] = v
                coef[1, q * 9 + n * 3 + m] = np.roll(v, 64)
    for m in range(3):
        v = np.repeat([w[2 * m], w[2 * m + 1]], 64)
        coef[0, 36 + m] = v
        coef[1, 36 + m] = np.roll(v, 64)
    coef = np.repeat(coef.reshape(78, 1, 128), 8, axis=1).astype(np.float32)

    to_sym = np.zeros((3, 128, 512))
    from_sym = np.zeros((256, 384))
    merge = np.zeros((128, 128))
    for i in range(5):
        for kp in range(6):
            base = i * 36 + kp * 6
            for c in range(3):
                merge[i * 18 + c * 6 + kp, c * 32 + 5 * i + kp] = 1.0
                for d in range(3):
                    s = base + sym_of(c, d)
                    targets = [(s, 2.0 if c == d else 1.0)]
                    if c == d:
                        targets += [(256 + base + q, 1.0) for q in range(3)]
                    for column, factor in targets:
                        if d < 2:
                            to_sym[d, c * 32 + 5 * i + kp, column] += factor
                        else:
                            for k in range(6):
                                to_sym[2, c * 32 + 5 * i + k, column] += factor * deriv[kp, k]
                    if d < 2:
                        from_sym[s, d * 128 + i * 18 + c * 6 + kp] += w[kp]
                    else:
                        for k in range(6):
                            from_sym[s, 256 + i * 18 + c * 6 + k] += w[kp] * deriv[kp, k]
    spread = np.zeros((128, 128))
    for piece in range(3):
        for k in range(NZ):
            for c in range(3):
                spread[piece * 32 + k, c * 32 + k] = 1.0
    of_first = np.tile(np.arange(PTS) < 36, 3)[None, :]
    back_el = np.concatenate([backward * of_first, backward * ~of_first], axis=0)
    wide = np.zeros((952, 512), np.float32)
    wide[0:384] = to_sym.reshape(384, 512)
    wide[384:640, 0:384] = from_sym
    wide[384:512, 384:512] = merge
    wide[640:832, 0:216] = back_el
    wide[640:952, 256:384] = coef[0:39].reshape(312, 128)
    wide[640:952, 384:512] = coef[39:78].reshape(312, 128)
    short = np.zeros((544, 256), ml_dtypes.bfloat16)
    short[0:216, 0:192] = forward2
    short[224:416, 0:216] = backward2
    short[416:544, 0:128] = spread
    return wide, short


def fdot(a, b):
    return jnp.dot(a, b, preferred_element_type=F32, precision=HIGHEST)


def bdot(a, b):
    return jnp.dot(a, b, preferred_element_type=F32)


def split(value):
    high = value.astype(BF16)
    return high, (value - high.astype(F32)).astype(BF16)


def fetch(pairs, sem):
    copies = [pltpu.make_async_copy(src, dst, sem.at[n]) for n, (src, dst) in enumerate(pairs)]
    for copy in copies:
        copy.start()
    return copies


def pack_kernel(*refs):
    sources, (x_ref, y_ref, c_ref, s_ref), (small, wide), sem = (
        refs[0:5],
        refs[5:9],
        refs[9:11],
        refs[11],
    )
    t_ref, d_ref, m_ref, mass_ref, id_ref = here = refs[12:17]
    copies = fetch(zip(sources, here, strict=True), sem)
    small[...] = jnp.zeros((NX, 16, SMALL), F32)
    for copy in copies[1:]:
        copy.wait()
    for x in range(NX):
        d = d_ref[x].astype(F32)
        m = m_ref[x].astype(F32)
        for c in range(3):
            small[x, 0:NY, 32 * c : 32 * c + NZ] = d[:, c, :]
            small[x, 0:NY, 128 + 32 * c : 128 + 32 * c + NZ] = m[:, c, :]
        small[x, 0:NY, 96 : 96 + NZ] = id_ref[x].astype(F32)
        rest = mass_ref[x]
        for piece in range(3):
            part = rest.astype(BF16).astype(F32)
            small[x, 0:NY, 256 + 32 * piece : 256 + 32 * piece + NZ] = part
            rest = rest - part
        s_ref[x] = small[x, 0:NY, :].astype(BF16)
    copies[0].wait()
    x_ref[:, :COLS] = t_ref[0]
    x_ref[:, COLS:] = small[0, 0:NY, :].astype(BF16)
    for x in range(NX):
        wide[x : x + 1, :COLS] = t_ref[x, 0:1, :].astype(F32)
        wide[x : x + 1, COLS:] = small[x, 0:1, :]
    y_ref[...] = wide[0:NX, :].astype(BF16)
    c_ref[...] = wide[0:1, :].astype(BF16)


def local_kernel(*refs):
    t_ref, tp_ref, d_ref, dp_ref, f_ref, wide_in, short_in = refs[0:7]
    base_ref, own_ref, copy_ref, wide_out, short_out = refs[7:12]
    own_ref[...] = jnp.zeros((2, NX, NY, 128), F32)
    wide_out[...] = wide_in[...]
    short_out[...] = short_in[...]
    for x in range(NX):
        now = t_ref[x]
        copy_ref[x] = now
        base_ref[x] = 2.0 * now.astype(F32) - tp_ref[x].astype(F32)
        d = 2.0 * d_ref[x].astype(F32) - dp_ref[x].astype(F32)
        f = f_ref[x].astype(F32)
        for c in range(3):
            own_ref[0, x, :, 32 * c : 32 * c + NZ] = d[:, c, :]
            own_ref[1, x, :, 32 * c : 32 * c + NZ] = f[:, c, :]


def main_kernel(
    n_x,
    n_y,
    par_ref,
    cell_ref,
    t_ref,
    base_ref,
    own_ref,
    s_ref,
    hx_ref,
    hy_ref,
    hc_ref,
    lanes_ref,
    dirs_ref,
    *rest,
):
    tab, short = rest[0:2]
    part_ref, rx_ref, ry_ref, rc_ref, share_ref = rest[2:7]
    (wide, uc, grad, stress, force, edge, amp) = rest[7:]

    for x in range(NX):
        wide[16 * x + 8 : 16 * x + 16, :] = jnp.zeros((8, WIDE), F32)
        wide[16 * x : 16 * x + NY, :COLS] = t_ref[x].astype(F32)
        wide[16 * x : 16 * x + NY, COLS:] = s_ref[x].astype(F32)
        wide[16 * x + NY : 16 * x + NY + 1, :] = hy_ref[x : x + 1, :].astype(F32)
    wide[88:96, :] = jnp.zeros((8, WIDE), F32)
    wide[80 : 80 + NY, :] = hx_ref[...].astype(F32)
    wide[80 + NY : 81 + NY, :] = hc_ref[...].astype(F32)

    low_rows = lax.broadcasted_iota(jnp.int32, (ROWS, 128), 1) < 64
    first_el = lax.broadcasted_iota(jnp.int32, (PTS, 128), 0) < 36
    first_el2 = lax.broadcasted_iota(jnp.int32, (PTS, 256), 0) < 36

    for i in range(5):
        odd = i % 2
        tile0 = (960 * i - 64 * odd) // 128

        def source(index, tile0=tile0):
            return wide[:, (tile0 + index) * 128 : (tile0 + index + 1) * 128]

        for m in range(3):
            t = [source(3 * m + q) for q in range(3 + odd)]
            if odd:
                by_c = (
                    jnp.where(low_rows, t[2], t[0]),
                    pltpu.roll(jnp.where(low_rows, t[1], t[2]), 64, 1),
                    jnp.where(low_rows, t[3], t[1]),
                )
            else:
                by_c = (
                    jnp.where(low_rows, t[0], t[1]),
                    pltpu.roll(jnp.where(low_rows, t[2], t[0]), 64, 1),
                    jnp.where(low_rows, t[1], t[2]),
                )
            for c in range(3):
                at = i * 1152 + (c * 3 + m) * 128
                value = by_c[c].astype(BF16)
                uc[0:ROWS, at : at + 128] = value
                uc[ROWS : 2 * ROWS, at : at + 128] = value

    fwd = short[0:216, 0:192]
    bwd = short[224:416, :]

    small_nodes = wide[:, COLS : COLS + 128].astype(BF16)
    pg = bdot(fwd, jnp.concatenate([small_nodes, small_nodes], axis=0))
    both = fdot(pg[0:PTS], tab[0:128, :])
    both = both + fdot(pg[PTS : 2 * PTS], tab[128:256, :])
    both = both + fdot(pg[2 * PTS : 3 * PTS], tab[256:384, :])
    lam_l = jnp.where(first_el2, lanes_ref[0:1, :], lanes_ref[1:2, :])
    mu_l = jnp.where(first_el2, lanes_ref[2:3, :], lanes_ref[3:4, :])
    primal_stress = lam_l * both[:, 256:512] + mu_l * both[:, 0:256]
    unit = fdot(both[:, 0:256], tab[384:640, 0:384])
    full = fdot(primal_stress, tab[384:640, 0:384])
    terms = jnp.zeros((2 * ROWS, 256), F32)
    for d in range(3):
        pair = jnp.concatenate([a[:, d * 128 : (d + 1) * 128] for a in (unit, full)], axis=1)
        terms = terms + fdot(tab[640:832, d * PTS : (d + 1) * PTS], pair)
    unit_first, unit_second = terms[0:ROWS, 0:128], terms[ROWS : 2 * ROWS, 0:128]
    primal_force = fdot(terms[0:ROWS, 128:256] + terms[ROWS : 2 * ROWS, 128:256], tab[384:512, 384:512])

    force[...] = jnp.zeros((ROWS, COLS), F32)
    lane = lax.broadcasted_iota(jnp.int32, (ROWS, 128), 1)
    row40 = lax.broadcasted_iota(jnp.int32, (40, 128), 0)
    half40 = lax.broadcasted_iota(jnp.int32, (40, 128), 1) // 64

    for i in range(5):
        odd = i % 2
        grad[...] = bdot(fwd, uc[:, i * 1152 : (i + 1) * 1152])
        lam_rows = jnp.where(first_el, par_ref[0, i], par_ref[0, 5 + i])
        mu_rows = jnp.where(first_el, par_ref[1, i], par_ref[1, 5 + i])
        edge[0:PTS, 0:128] = lam_rows
        edge[0:PTS, 128:256] = mu_rows
        pick = [
            jnp.where(dirs_ref[...] == cell_ref[0, 5 * e + i], 1.0, 0.0) for e in range(2)
        ]
        for c in range(3):
            for m in range(3):
                target = c * 6 + 2 * m + (1 - half40 if odd else half40)
                value = jnp.where(
                    row40 == target,
                    pick[0],
                    jnp.where(row40 == target + 18, pick[1], 0.0),
                )
                stress[216:256, (c * 3 + m) * 128 : (c * 3 + m + 1) * 128] = value

        def rows_step(rc, carry, odd=odd):
            row = pl.multiple_of(rc * 8, 8)

            def tile(kind, c, m):
                at = pl.multiple_of(kind * PTS + rc * 8, 8)
                return grad[pl.ds(at, 8), (c * 3 + m) * 128 : (c * 3 + m + 1) * 128]

            def coef(index):
                at = 256 + 128 * odd
                return tab[640 + 8 * index : 648 + 8 * index, at : at + 128]

            def put(direction, c, m, value):
                at = pl.multiple_of(direction * PTS + rc * 8, 8)
                stress[pl.ds(at, 8), (c * 3 + m) * 128 : (c * 3 + m + 1) * 128] = value

            def along_z(tiles, offset):
                turned = [pltpu.roll(v, 64, 1) for v in tiles]
                return [
                    sum(
                        coef(offset + n * 3 + m) * tiles[m]
                        + coef(offset + 9 + n * 3 + m) * turned[m]
                        for m in range(3)
                    )
                    for n in range(3)
                ]

            gz = [along_z([tile(2, c, m) for m in range(3)], 0) for c in range(3)]
            lam = edge[pl.ds(row, 8), 0:128]
            mu = edge[pl.ds(row, 8), 128:256]
            z_stress = [[None] * 3 for _ in range(3)]
            for m in range(3):
                wz = coef(36 + m)
                muw = mu * wz
                g = [[tile(0, c, m) for c in range(3)], [tile(1, c, m) for c in range(3)]]
                g.append([gz[c][m] for c in range(3)])
                dil = (lam * wz) * (g[0][0] + g[1][1] + g[2][2])
                put(0, 0, m, (muw + muw) * g[0][0] + dil)
                put(1, 1, m, (muw + muw) * g[1][1] + dil)
                z_stress[2][m] = (muw + muw) * g[2][2] + dil
                value = muw * (g[0][1] + g[1][0])
                put(0, 1, m, value)
                put(1, 0, m, value)
                value = muw * (g[0][2] + g[2][0])
                put(0, 2, m, value)
                z_stress[0][m] = value
                value = muw * (g[1][2] + g[2][1])
                put(1, 2, m, value)
                z_stress[1][m] = value
            for c in range(3):
                for n, value in enumerate(along_z(z_stress[c], 18)):
                    put(2, c, n, value)
            return carry

        lax.fori_loop(0, 9, rows_step, 0, unroll=UNROLL)
        s_high = stress[...].astype(BF16)
        s_low = (stress[0:216, :] - s_high[0:216].astype(F32)).astype(BF16)
        unit_here = jnp.where(
            lane < 106,
            pltpu.roll(unit_first, (88 - 18 * i) % 128, 1),
            pltpu.roll(unit_second, (106 - 18 * i) % 128, 1),
        )
        unit_high, unit_low = split(unit_here)
        unit_both = jnp.concatenate([unit_high, unit_low], axis=0)
        lane2 = lax.broadcasted_iota(jnp.int32, (2 * ROWS, 128), 1)
        inside = (lane2 >= 88) & (lane2 < 124)
        left = jnp.concatenate(
            [
                bwd[:, 0:128],
                jnp.where(inside, unit_both.astype(F32), bwd[:, 128:256].astype(F32)).astype(BF16),
            ],
            axis=1,
        )
        two = bdot(left, s_high)
        nodes = two[0:ROWS] + two[ROWS : 2 * ROWS] + bdot(bwd[0:ROWS, 0:216], s_low)

        def node_tile(c, m, nodes=nodes):
            return nodes[:, (c * 3 + m) * 128 : (c * 3 + m + 1) * 128]

        tile0 = (960 * i - 64 * odd) // 128

        def add(index, value, tile0=tile0):
            at = (tile0 + index) * 128
            force[:, at : at + 128] = force[:, at : at + 128] + value

        zero = jnp.zeros((ROWS, 128), F32)
        last_c2 = zero
        for m in range(3):
            c0, c2 = node_tile(0, m), node_tile(2, m)
            c1 = pltpu.roll(node_tile(1, m), 64, 1)
            if odd:
                add(3 * m, jnp.where(low_rows, last_c2, c0))
                add(3 * m + 1, jnp.where(low_rows, c1, c2))
                add(3 * m + 2, jnp.where(low_rows, c0, c1))
                last_c2 = c2
            else:
                add(3 * m, jnp.where(low_rows, c0, c1))
                add(3 * m + 1, jnp.where(low_rows, c2, c0))
                add(3 * m + 2, jnp.where(low_rows, c1, c2))
        if odd:
            add(9, jnp.where(low_rows, last_c2, zero))

    mass = bdot(wide[:, COLS + 256 : COLS + 384].astype(BF16), short[416:544, 0:128])
    rate = STEP_SQUARED / jnp.where(mass > 0.0, mass, 1.0)
    primal_step = -rate * primal_force
    for x in range(NX):
        part_ref[x, :, COLS:] = (
            primal_step[16 * x : 16 * x + NY, :]
            + own_ref[0, x]
            + rate[16 * x : 16 * x + NY, :] * own_ref[1, x]
        )
    rx_ref[:, COLS:] = primal_step[80 : 80 + NY, :].astype(BF16)
    for x in range(NX):
        edge[x : x + 1, COLS:BACK] = primal_step[16 * x + NY : 16 * x + NY + 1, :]
    rc_ref[:, COLS:] = primal_step[80 + NY : 81 + NY, :].astype(BF16)

    ids = jnp.transpose(wide[:, COLS : COLS + 128])[96:128]
    ids = jnp.concatenate([ids, ids], axis=1)
    modes = jnp.transpose(wide[:, COLS + 128 : COLS + 256])
    modes = jnp.concatenate([modes, modes], axis=1)
    port = lax.broadcasted_iota(jnp.int32, (PORTS, 2 * ROWS), 0).astype(F32)
    total = jnp.zeros((128, 128), F32)
    for tile in range(39):
        at = slice(tile * 128, (tile + 1) * 128)
        two_halves = [divmod(2 * tile, 3), divmod(2 * tile + 1, 3)]
        k0, k1 = two_halves[0][0], two_halves[1][0]
        r0 = jnp.broadcast_to(rate[:, k0 : k0 + 1], (ROWS, 128))
        if k1 != k0:
            r1 = jnp.broadcast_to(rate[:, k1 : k1 + 1], (ROWS, 128))
            r0 = jnp.where(low_rows, r0, r1)
        force[:, at] = -r0 * force[:, at]
        for x in range(NX):
            rows = slice(16 * x, 16 * x + NY)
            now = force[rows, at] + base_ref[x, :, at]
            force[rows, at] = now
            part_ref[x, :, at] = now
        high, low = split(force[:, at])
        picked = [
            jnp.where(ids[k : k + 1, :] == port, modes[32 * c + k : 32 * c + k + 1, :], 0.0)
            for k, c in two_halves
        ]
        left = jnp.concatenate(picked, axis=0).astype(BF16)
        total = total + bdot(left, jnp.concatenate([high, low], axis=0))
    rx_ref[:, :COLS] = force[80 : 80 + NY, :].astype(BF16)
    for x in range(NX):
        edge[x : x + 1, :COLS] = force[16 * x + NY : 16 * x + NY + 1, :]
    ry_ref[...] = edge[0:NX, 0:BACK].astype(BF16)
    rc_ref[:, :COLS] = force[80 + NY : 81 + NY, :].astype(BF16)
    amp[:, 0:64] = total[0:64, 0:64] + pltpu.roll(total[64:128, :], 64, 1)[:, 0:64]
    p_rows, p_cols = PORTS // n_y, 64 // n_x
    for q in range(p_rows):
        mine = amp[pl.ds(q, n_y, stride=p_rows), :] if p_rows > 1 else amp[...]
        for a in range(n_x):
            share_ref[a * n_y : (a + 1) * n_y, q * p_cols : (q + 1) * p_cols] = mine[
                :, a * p_cols : (a + 1) * p_cols
            ]


def last_kernel(part_ref, rx_ref, ry_ref, rc_ref, t_ref, d_ref):
    first = lax.broadcasted_iota(jnp.int32, (NY, BACK), 0) == 0
    for x in range(NX):
        row = ry_ref[x : x + 1, :].astype(F32)
        if x == 0:
            row = row + rc_ref[...].astype(F32)
        value = part_ref[x] + jnp.where(first, row, 0.0)
        if x == 0:
            value = value + rx_ref[...].astype(F32)
        t_ref[x] = value[:, :COLS].astype(BF16)
        d_ref[x] = value[:, COLS:]


def final_kernel(port_rows, port_cols, share_ref, d_ref, amp_ref, out_ref, lined):
    row = jnp.sum(share_ref[...], axis=0, keepdims=True)
    for q in range(port_rows):
        amp_ref[q : q + 1, :] = row[:, q * port_cols : (q + 1) * port_cols]
    for x in range(NX):
        for c in range(3):
            lined[x, :, c, :] = d_ref[x, :, 32 * c : 32 * c + NZ]
        out_ref[x] = lined[x].astype(BF16)


def per_device(
    disp,
    disp_prev,
    tangent,
    tangent_prev,
    lame_lambda,
    lame_mu,
    node_mass,
    force,
    cell_block,
    direction_block,
    port_id,
    port_mode,
):
    tab = tables()
    nx_dev, ny_dev = lax.axis_size("gx"), lax.axis_size("gy")
    vmem = pl.BlockSpec(memory_space=pltpu.VMEM)
    smem = pl.BlockSpec(memory_space=pltpu.SMEM)
    hbm = pl.BlockSpec(memory_space=pltpu.HBM)
    params = pltpu.CompilerParams(vmem_limit_bytes=VMEM_LIMIT)

    def step(shift_x, shift_y):
        route = []
        for i in range(nx_dev):
            for j in range(ny_dev):
                a, b = i + shift_x, j + shift_y
                if 0 <= a < nx_dev and 0 <= b < ny_dev:
                    route.append((i * ny_dev + j, a * ny_dev + b))
        return route

    def send(block, shift_x, shift_y):
        return lax.ppermute(block, ("gx", "gy"), step(shift_x, shift_y))

    by_comp = [a.transpose(0, 1, 3, 2) for a in (disp, port_mode, disp_prev, force)]
    face_x, face_y, corner, small = pl.pallas_call(
        pack_kernel,
        out_shape=(
            jax.ShapeDtypeStruct((NY, WIDE), BF16),
            jax.ShapeDtypeStruct((NX, WIDE), BF16),
            jax.ShapeDtypeStruct((1, WIDE), BF16),
            jax.ShapeDtypeStruct((NX, NY, SMALL), BF16),
        ),
        in_specs=[hbm] * 5,
        out_specs=(vmem,) * 4,
        scratch_shapes=[
            pltpu.VMEM((NX, 16, SMALL), F32),
            pltpu.VMEM((8, WIDE), F32),
            pltpu.SemaphoreType.DMA((5,)),
            pltpu.VMEM((NX, NY, COLS), BF16),
            pltpu.VMEM((NX, NY, 3, NZ), BF16),
            pltpu.VMEM((NX, NY, 3, NZ), BF16),
            pltpu.VMEM((NX, NY, NZ), F32),
            pltpu.VMEM((NX, NY, NZ), jnp.int32),
        ],
        compiler_params=pltpu.CompilerParams(vmem_limit_bytes=VMEM_MOST),
    )(tangent, by_comp[0], by_comp[1], node_mass, port_id)
    halo_x = send(face_x, -1, 0)
    halo_y = send(face_y, 0, -1)
    halo_c = send(corner, -1, -1)

    wide_table, short_table = (jnp.asarray(a) for a in tab)
    base, own, near, *near_tables = pl.pallas_call(
        local_kernel,
        out_shape=(
            jax.ShapeDtypeStruct((NX, NY, COLS), F32),
            jax.ShapeDtypeStruct((2, NX, NY, 128), F32),
            jax.ShapeDtypeStruct((NX, NY, COLS), BF16),
            jax.ShapeDtypeStruct(wide_table.shape, F32),
            jax.ShapeDtypeStruct(short_table.shape, BF16),
        ),
        in_specs=[vmem] * 7,
        out_specs=(vmem,) * 5,
        compiler_params=params,
        cost_estimate=pl.CostEstimate(
            flops=LONG_FLOPS, bytes_accessed=LONG_BYTES, transcendentals=0
        ),
    )(tangent, tangent_prev, by_comp[0], by_comp[2], by_comp[3], wide_table, short_table)

    par = jnp.stack([lame_lambda.reshape(10), lame_mu.reshape(10)]).astype(F32)
    cells = cell_block.reshape(1, 10)
    by_lane = jnp.repeat(par.reshape(4, 5), 36, axis=1)
    by_lane = jnp.pad(by_lane, ((0, 0), (0, 76)))
    dirs = jnp.concatenate([direction_block, direction_block]).reshape(1, 128)

    part, ret_x, ret_y, ret_c, shares = pl.pallas_call(
        functools.partial(main_kernel, nx_dev, ny_dev),
        out_shape=(
            jax.ShapeDtypeStruct((NX, NY, BACK), F32),
            jax.ShapeDtypeStruct((NY, BACK), BF16),
            jax.ShapeDtypeStruct((NX, BACK), BF16),
            jax.ShapeDtypeStruct((1, BACK), BF16),
            jax.ShapeDtypeStruct((nx_dev * ny_dev, PORTS * 64 // (nx_dev * ny_dev)), F32),
        ),
        in_specs=[smem, smem]
        + [vmem] * 11,
        out_specs=(vmem,) * 5,
        scratch_shapes=[
            pltpu.VMEM((ROWS, WIDE), F32),
            pltpu.VMEM((2 * ROWS, 5 * 1152), BF16),
            pltpu.VMEM((3 * PTS, 1152), F32),
            pltpu.VMEM((256, 1152), F32),
            pltpu.VMEM((ROWS, COLS), F32),
            pltpu.VMEM((PTS, BACK), F32),
            pltpu.VMEM((PORTS, 64), F32),
        ],
        compiler_params=params,
        cost_estimate=pl.CostEstimate(
            flops=400000000, bytes_accessed=8000000, transcendentals=0
        ),
    )(
        par,
        cells,
        near,
        base,
        own,
        small,
        halo_x,
        halo_y,
        halo_c,
        by_lane,
        dirs,
        *near_tables,
    )

    port_rows, port_cols = PORTS // ny_dev, 64 // nx_dev
    shares = lax.all_to_all(shares, ("gx", "gy"), 0, 0)
    back_c = send(ret_c, 1, 1)
    back_y = send(ret_y, 0, 1)
    back_x = send(ret_x, 1, 0)

    tangent_next, disp_wide = pl.pallas_call(
        last_kernel,
        out_shape=(
            jax.ShapeDtypeStruct((NX, NY, COLS), BF16),
            jax.ShapeDtypeStruct((NX, NY, 128), F32),
        ),
        in_specs=[vmem] * 4,
        out_specs=(vmem, vmem),
        compiler_params=params,
        cost_estimate=pl.CostEstimate(flops=4000000, bytes_accessed=8000000, transcendentals=0),
    )(part, back_x, back_y, back_c)
    port_amp, disp_next = pl.pallas_call(
        functools.partial(final_kernel, port_rows, port_cols),
        out_shape=(
            jax.ShapeDtypeStruct((port_rows, port_cols), F32),
            jax.ShapeDtypeStruct((NX, NY, 3, NZ), BF16),
        ),
        in_specs=[vmem, vmem],
        out_specs=(vmem, vmem),
        scratch_shapes=[pltpu.VMEM((NX, NY, 3, NZ), F32)],
        compiler_params=params,
    )(shares, disp_wide)
    return (disp_next.transpose(0, 1, 3, 2), tangent_next, port_amp)


def solution(mesh):
    return jax.shard_map(
        per_device,
        mesh=mesh,
        in_specs=(
            P("gx", "gy", None, None),
            P("gx", "gy", None, None),
            P("gx", "gy", None),
            P("gx", "gy", None),
            P("gx", "gy", None),
            P("gx", "gy", None),
            P("gx", "gy", None),
            P("gx", "gy", None, None),
            P("gx", "gy", None),
            P(),
            P("gx", "gy", None),
            P("gx", "gy", None, None),
        ),
        out_specs=(P("gx", "gy", None, None), P("gx", "gy", None), P("gy", "gx")),
        check_vma=False,
    )
```

```python
import functools

import jax
import jax.numpy as jnp
import ml_dtypes
import numpy as np
from jax import lax
from jax.experimental import pallas as pl
from jax.experimental.pallas import tpu as pltpu
from jax.sharding import PartitionSpec as P

PORTS = 64
GLL_POINTS = np.array(
    [-1.0, -0.765055323929465, -0.285231516480645, 0.285231516480645, 0.765055323929465, 1.0]
)
GLL_WEIGHTS = np.array(
    [
        1.0 / 15.0,
        0.378474956297847,
        0.554858377035486,
        0.554858377035486,
        0.378474956297847,
        1.0 / 15.0,
    ]
)
STEP_SQUARED = 0.03
F32 = jnp.float32
BF16 = jnp.bfloat16

NX, NY, NZ = 5, 10, 26
COLS = 4992
SMALL = 384
WIDE = COLS + SMALL
BACK = COLS + 128
ROWS = 96
PTS = 72
VMEM_LIMIT = 24 * 1024 * 1024
VMEM_MOST = 60 * 1024 * 1024
UNROLL = 9
CORNER = 1
SHARE = 64


def derivative_table():
    identity = np.eye(6)
    differences = GLL_POINTS[:, None] - GLL_POINTS[None, :] + identity
    barycentric = 1.0 / np.prod(differences, axis=1)
    matrix = barycentric[None, :] / barycentric[:, None] / differences
    matrix = matrix * (1.0 - identity)
    matrix = matrix - identity * matrix.sum(axis=1)[:, None]
    return matrix


def halves(matrix):
    matrix = matrix.astype(np.float32)
    high = matrix.astype(ml_dtypes.bfloat16)
    low = (matrix - high.astype(np.float32)).astype(ml_dtypes.bfloat16)
    return high, low


SYM = {(0, 0): 0, (1, 1): 1, (2, 2): 2, (0, 1): 3, (0, 2): 4, (1, 2): 5}


def sym_of(c, d):
    return SYM[(min(c, d), max(c, d))]


@functools.cache
def tables():
    deriv = derivative_table()
    w = GLL_WEIGHTS
    fx = np.zeros((PTS, ROWS))
    fy = np.zeros((PTS, ROWS))
    fv = np.zeros((PTS, ROWS))
    wxy = np.zeros(PTS)
    for e in range(2):
        for px in range(6):
            for py in range(6):
                r = e * 36 + px * 6 + py
                wxy[r] = w[px] * w[py]
                fv[r, 16 * px + 5 * e + py] = 1.0
                for a in range(6):
                    fx[r, 16 * a + 5 * e + py] += deriv[px, a]
                    fy[r, 16 * px + 5 * e + a] += deriv[py, a]
    forward = np.concatenate([fx, fy, fv], axis=0)
    f_high, f_low = halves(forward)
    forward2 = np.concatenate([f_high, f_low], axis=1)
    backward = np.concatenate([(m * wxy[:, None]).T for m in (fx, fy, fv)], axis=1)
    b_high, b_low = halves(backward)
    backward2 = np.concatenate([b_high, b_low], axis=0)

    coef = np.zeros((2, 39, 128))
    for n in range(3):
        for m in range(3):
            a = np.repeat([deriv[2 * n, 2 * m], deriv[2 * n + 1, 2 * m + 1]], 64)
            b = np.repeat([deriv[2 * n, 2 * m + 1], deriv[2 * n + 1, 2 * m]], 64)
            at = np.repeat([deriv[2 * m, 2 * n], deriv[2 * m + 1, 2 * n + 1]], 64)
            bt = np.repeat([deriv[2 * m + 1, 2 * n], deriv[2 * m, 2 * n + 1]], 64)
            for q, v in enumerate((a, b, at, bt)):
                coef[0, q * 9 + n * 3 + m] = v
                coef[1, q * 9 + n * 3 + m] = np.roll(v, 64)
    for m in range(3):
        v = np.repeat([w[2 * m], w[2 * m + 1]], 64)
        coef[0, 36 + m] = v
        coef[1, 36 + m] = np.roll(v, 64)
    coef = np.repeat(coef.reshape(78, 1, 128), 8, axis=1).astype(np.float32)

    to_sym = np.zeros((3, 128, 512))
    from_sym = np.zeros((256, 384))
    merge = np.zeros((128, 128))
    for i in range(5):
        for kp in range(6):
            base = i * 36 + kp * 6
            for c in range(3):
                merge[i * 18 + c * 6 + kp, c * 32 + 5 * i + kp] = 1.0
                for d in range(3):
                    s = base + sym_of(c, d)
                    targets = [(s, 2.0 if c == d else 1.0)]
                    if c == d:
                        targets += [(256 + base + q, 1.0) for q in range(3)]
                    for column, factor in targets:
                        if d < 2:
                            to_sym[d, c * 32 + 5 * i + kp, column] += factor
                        else:
                            for k in range(6):
                                to_sym[2, c * 32 + 5 * i + k, column] += factor * deriv[kp, k]
                    if d < 2:
                        from_sym[s, d * 128 + i * 18 + c * 6 + kp] += w[kp]
                    else:
                        for k in range(6):
                            from_sym[s, 256 + i * 18 + c * 6 + k] += w[kp] * deriv[kp, k]
    spread = np.zeros((128, 128))
    for piece in range(3):
        for k in range(NZ):
            for c in range(3):
                spread[piece * 32 + k, c * 32 + k] = 1.0
    of_first = np.tile(np.arange(PTS) < 36, 3)[None, :]
    back_el = np.concatenate([backward * of_first, backward * ~of_first], axis=0)
    wide = np.zeros((952, 512), np.float32)
    wide[0:384] = to_sym.reshape(384, 512)
    wide[384:640, 0:384] = from_sym
    wide[384:512, 384:512] = merge
    wide[640:832, 0:216] = back_el
    wide[640:952, 256:384] = coef[0:39].reshape(312, 128)
    wide[640:952, 384:512] = coef[39:78].reshape(312, 128)
    short = np.zeros((544, 256), ml_dtypes.bfloat16)
    short[0:216, 0:192] = forward2
    short[224:416, 0:216] = backward2
    short[416:544, 0:128] = spread
    return wide, short


def fdot(a, b):
    (a_high, a_low), (b_high, b_low) = split(a), split(b)
    return bdot(a_high, b_high) + (bdot(a_low, b_high) + bdot(a_high, b_low))


def bdot(a, b):
    return jnp.dot(a, b, preferred_element_type=F32)


def split(value):
    high = value.astype(BF16)
    return high, (value - high.astype(F32)).astype(BF16)


def fetch(pairs, sem):
    copies = [pltpu.make_async_copy(src, dst, sem.at[n]) for n, (src, dst) in enumerate(pairs)]
    for copy in copies:
        copy.start()
    return copies


def pack_kernel(*refs):
    sources, (x_ref, y_ref, c_ref, s_ref, own_ref, par_ref) = refs[0:11], refs[11:17]
    small, wide, sem = refs[17:20]
    here = refs[20:]
    t_ref, d_ref, m_ref, mass_ref, id_ref, dp_ref, f_ref, lam_ref, mu_ref, cell_ref, dir_ref = here
    copies = fetch(zip(sources, here, strict=True), sem)
    small[...] = jnp.zeros((NX, 16, SMALL), F32)
    own_ref[...] = jnp.zeros((2, NX, NY, 128), F32)
    for copy in copies[1:]:
        copy.wait()
    for x in range(NX):
        d = d_ref[x].astype(F32)
        m = m_ref[x].astype(F32)
        before = 2.0 * d - dp_ref[x].astype(F32)
        f = f_ref[x].astype(F32)
        for c in range(3):
            small[x, 0:NY, 32 * c : 32 * c + NZ] = d[:, c, :]
            small[x, 0:NY, 128 + 32 * c : 128 + 32 * c + NZ] = m[:, c, :]
            own_ref[0, x, :, 32 * c : 32 * c + NZ] = before[:, c, :]
            own_ref[1, x, :, 32 * c : 32 * c + NZ] = f[:, c, :]
        small[x, 0:NY, 96 : 96 + NZ] = id_ref[x].astype(F32)
        rest = mass_ref[x]
        for piece in range(3):
            part = rest.astype(BF16).astype(F32)
            small[x, 0:NY, 256 + 32 * piece : 256 + 32 * piece + NZ] = part
            rest = rest - part
        s_ref[x] = small[x, 0:NY, :].astype(BF16)
    along_z = lax.broadcasted_iota(jnp.int32, (1, 256), 1) // 36
    for q, ref in enumerate((lam_ref, mu_ref)):
        values = ref[0].astype(F32)
        for e in range(2):
            row = jnp.zeros((1, 256), F32)
            for i in range(5):
                row = jnp.where(
                    along_z == i, jnp.broadcast_to(values[e : e + 1, i : i + 1], (1, 256)), row
                )
            par_ref[2 * q + e : 2 * q + e + 1, :] = row
    dirs = jnp.concatenate([dir_ref[...], dir_ref[...]], axis=1)
    cells = cell_ref[0]
    for e in range(2):
        for i in range(5):
            same = dirs == jnp.broadcast_to(cells[e : e + 1, i : i + 1], (1, 128))
            par_ref[8 + 5 * e + i : 9 + 5 * e + i, 0:128] = jnp.where(same, 1.0, 0.0)
    copies[0].wait()
    x_ref[:, :COLS] = t_ref[0]
    x_ref[:, COLS:] = small[0, 0:NY, :].astype(BF16)
    for x in range(NX):
        wide[x : x + 1, :COLS] = t_ref[x, 0:1, :].astype(F32)
        wide[x : x + 1, COLS:] = small[x, 0:1, :]
    y_ref[...] = wide[0:NX, :].astype(BF16)
    c_ref[...] = wide[0:1, :].astype(BF16)


def local_kernel(t_ref, tp_ref, wide_in, short_in, base_ref, copy_ref, wide_out, short_out):
    wide_out[...] = wide_in[...]
    short_out[...] = short_in[...]
    for x in range(NX):
        now = t_ref[x]
        copy_ref[x] = now
        base_ref[x] = 2.0 * now.astype(F32) - tp_ref[x].astype(F32)


def main_kernel(
    n_x,
    n_y,
    par_ref,
    t_ref,
    base_ref,
    own_ref,
    s_ref,
    hx_ref,
    hy_ref,
    hc_ref,
    *rest,
):
    tab, short = rest[0:2]
    part_ref, rx_ref, ry_ref, rc_ref, share_ref = rest[2:7]
    (wide, uc, grad, stress, force, edge, amp) = rest[7:]

    for x in range(NX):
        wide[16 * x + 8 : 16 * x + 16, :] = jnp.zeros((8, WIDE), F32)
        wide[16 * x : 16 * x + NY, :COLS] = t_ref[x].astype(F32)
        wide[16 * x : 16 * x + NY, COLS:] = s_ref[x].astype(F32)
        wide[16 * x + NY : 16 * x + NY + 1, :] = hy_ref[x : x + 1, :].astype(F32)
    wide[88:96, :] = jnp.zeros((8, WIDE), F32)
    wide[80 : 80 + NY, :] = hx_ref[...].astype(F32)
    wide[80 + NY : 81 + NY, :] = hc_ref[...].astype(F32)

    low_rows = lax.broadcasted_iota(jnp.int32, (ROWS, 128), 1) < 64
    first_el = lax.broadcasted_iota(jnp.int32, (PTS, 128), 0) < 36
    first_el2 = lax.broadcasted_iota(jnp.int32, (PTS, 256), 0) < 36

    for i in range(5):
        odd = i % 2
        tile0 = (960 * i - 64 * odd) // 128

        def source(index, tile0=tile0):
            return wide[:, (tile0 + index) * 128 : (tile0 + index + 1) * 128]

        for m in range(3):
            t = [source(3 * m + q) for q in range(3 + odd)]
            if odd:
                by_c = (
                    jnp.where(low_rows, t[2], t[0]),
                    pltpu.roll(jnp.where(low_rows, t[1], t[2]), 64, 1),
                    jnp.where(low_rows, t[3], t[1]),
                )
            else:
                by_c = (
                    jnp.where(low_rows, t[0], t[1]),
                    pltpu.roll(jnp.where(low_rows, t[2], t[0]), 64, 1),
                    jnp.where(low_rows, t[1], t[2]),
                )
            for c in range(3):
                at = i * 1152 + (c * 3 + m) * 128
                value = by_c[c].astype(BF16)
                uc[0:ROWS, at : at + 128] = value
                uc[ROWS : 2 * ROWS, at : at + 128] = value

    fwd = short[0:216, 0:192]
    bwd = short[224:416, :]

    small_nodes = wide[:, COLS : COLS + 128].astype(BF16)
    pg = bdot(fwd, jnp.concatenate([small_nodes, small_nodes], axis=0))
    both = fdot(pg[0:PTS], tab[0:128, :])
    both = both + fdot(pg[PTS : 2 * PTS], tab[128:256, :])
    both = both + fdot(pg[2 * PTS : 3 * PTS], tab[256:384, :])
    lam_l = jnp.where(first_el2, par_ref[0:1, :], par_ref[1:2, :])
    mu_l = jnp.where(first_el2, par_ref[2:3, :], par_ref[3:4, :])
    primal_stress = lam_l * both[:, 256:512] + mu_l * both[:, 0:256]
    unit = fdot(both[:, 0:256], tab[384:640, 0:384])
    full = fdot(primal_stress, tab[384:640, 0:384])
    terms = jnp.zeros((2 * ROWS, 256), F32)
    for d in range(3):
        pair = jnp.concatenate([a[:, d * 128 : (d + 1) * 128] for a in (unit, full)], axis=1)
        terms = terms + fdot(tab[640:832, d * PTS : (d + 1) * PTS], pair)
    unit_first, unit_second = terms[0:ROWS, 0:128], terms[ROWS : 2 * ROWS, 0:128]
    primal_force = fdot(terms[0:ROWS, 128:256] + terms[ROWS : 2 * ROWS, 128:256], tab[384:512, 384:512])

    force[...] = jnp.zeros((ROWS, COLS), F32)
    lane = lax.broadcasted_iota(jnp.int32, (ROWS, 128), 1)
    row40 = lax.broadcasted_iota(jnp.int32, (40, 128), 0)
    half40 = lax.broadcasted_iota(jnp.int32, (40, 128), 1) // 64

    for i in range(5):
        odd = i % 2
        grad[...] = bdot(fwd, uc[:, i * 1152 : (i + 1) * 1152])
        lam_rows, mu_rows = (
            jnp.where(
                first_el,
                *(
                    jnp.broadcast_to(par_ref[r : r + 1, 36 * i : 36 * i + 1], (PTS, 128))
                    for r in (q, q + 1)
                ),
            )
            for q in (0, 2)
        )
        edge[0:PTS, 0:128] = lam_rows
        edge[0:PTS, 128:256] = mu_rows
        pick = [par_ref[8 + 5 * e + i : 9 + 5 * e + i, 0:128] for e in range(2)]
        for c in range(3):
            for m in range(3):
                target = c * 6 + 2 * m + (1 - half40 if odd else half40)
                value = jnp.where(
                    row40 == target,
                    pick[0],
                    jnp.where(row40 == target + 18, pick[1], 0.0),
                )
                stress[216:256, (c * 3 + m) * 128 : (c * 3 + m + 1) * 128] = value

        def rows_step(rc, carry, odd=odd):
            row = pl.multiple_of(rc * 8, 8)

            def tile(kind, c, m):
                at = pl.multiple_of(kind * PTS + rc * 8, 8)
                return grad[pl.ds(at, 8), (c * 3 + m) * 128 : (c * 3 + m + 1) * 128]

            def coef(index):
                at = 256 + 128 * odd
                return tab[640 + 8 * index : 648 + 8 * index, at : at + 128]

            def put(direction, c, m, value):
                at = pl.multiple_of(direction * PTS + rc * 8, 8)
                stress[pl.ds(at, 8), (c * 3 + m) * 128 : (c * 3 + m + 1) * 128] = value

            def along_z(tiles, offset):
                turned = [pltpu.roll(v, 64, 1) for v in tiles]
                return [
                    sum(
                        coef(offset + n * 3 + m) * tiles[m]
                        + coef(offset + 9 + n * 3 + m) * turned[m]
                        for m in range(3)
                    )
                    for n in range(3)
                ]

            gz = [along_z([tile(2, c, m) for m in range(3)], 0) for c in range(3)]
            lam = edge[pl.ds(row, 8), 0:128]
            mu = edge[pl.ds(row, 8), 128:256]
            z_stress = [[None] * 3 for _ in range(3)]
            for m in range(3):
                wz = coef(36 + m)
                muw = mu * wz
                g = [[tile(0, c, m) for c in range(3)], [tile(1, c, m) for c in range(3)]]
                g.append([gz[c][m] for c in range(3)])
                dil = (lam * wz) * (g[0][0] + g[1][1] + g[2][2])
                put(0, 0, m, (muw + muw) * g[0][0] + dil)
                put(1, 1, m, (muw + muw) * g[1][1] + dil)
                z_stress[2][m] = (muw + muw) * g[2][2] + dil
                value = muw * (g[0][1] + g[1][0])
                put(0, 1, m, value)
                put(1, 0, m, value)
                value = muw * (g[0][2] + g[2][0])
                put(0, 2, m, value)
                z_stress[0][m] = value
                value = muw * (g[1][2] + g[2][1])
                put(1, 2, m, value)
                z_stress[1][m] = value
            for c in range(3):
                for n, value in enumerate(along_z(z_stress[c], 18)):
                    put(2, c, n, value)
            return carry

        lax.fori_loop(0, 9, rows_step, 0, unroll=UNROLL)
        s_high = stress[...].astype(BF16)
        s_low = (stress[0:216, :] - s_high[0:216].astype(F32)).astype(BF16)
        unit_here = jnp.where(
            lane < 106,
            pltpu.roll(unit_first, (88 - 18 * i) % 128, 1),
            pltpu.roll(unit_second, (106 - 18 * i) % 128, 1),
        )
        unit_high, unit_low = split(unit_here)
        unit_both = jnp.concatenate([unit_high, unit_low], axis=0)
        lane2 = lax.broadcasted_iota(jnp.int32, (2 * ROWS, 128), 1)
        inside = (lane2 >= 88) & (lane2 < 124)
        left = jnp.concatenate(
            [
                bwd[:, 0:128],
                jnp.where(inside, unit_both.astype(F32), bwd[:, 128:256].astype(F32)).astype(BF16),
            ],
            axis=1,
        )
        two = bdot(left, s_high)
        nodes = two[0:ROWS] + two[ROWS : 2 * ROWS] + bdot(bwd[0:ROWS, 0:216], s_low)

        def node_tile(c, m, nodes=nodes):
            return nodes[:, (c * 3 + m) * 128 : (c * 3 + m + 1) * 128]

        tile0 = (960 * i - 64 * odd) // 128

        def add(index, value, tile0=tile0):
            at = (tile0 + index) * 128
            force[:, at : at + 128] = force[:, at : at + 128] + value

        zero = jnp.zeros((ROWS, 128), F32)
        last_c2 = zero
        for m in range(3):
            c0, c2 = node_tile(0, m), node_tile(2, m)
            c1 = pltpu.roll(node_tile(1, m), 64, 1)
            if odd:
                add(3 * m, jnp.where(low_rows, last_c2, c0))
                add(3 * m + 1, jnp.where(low_rows, c1, c2))
                add(3 * m + 2, jnp.where(low_rows, c0, c1))
                last_c2 = c2
            else:
                add(3 * m, jnp.where(low_rows, c0, c1))
                add(3 * m + 1, jnp.where(low_rows, c2, c0))
                add(3 * m + 2, jnp.where(low_rows, c1, c2))
        if odd:
            add(9, jnp.where(low_rows, last_c2, zero))

    mass = bdot(wide[:, COLS + 256 : COLS + 384].astype(BF16), short[416:544, 0:128])
    rate = STEP_SQUARED / jnp.where(mass > 0.0, mass, 1.0)
    primal_step = -rate * primal_force
    for x in range(NX):
        part_ref[x, :, COLS:] = (
            primal_step[16 * x : 16 * x + NY, :]
            + own_ref[0, x]
            + rate[16 * x : 16 * x + NY, :] * own_ref[1, x]
        )
    rx_ref[:, COLS:] = primal_step[80 : 80 + NY, :].astype(BF16)
    for x in range(NX):
        edge[x : x + 1, COLS:BACK] = primal_step[16 * x + NY : 16 * x + NY + 1, :]
    rc_ref[:, COLS:] = jnp.broadcast_to(primal_step[80 + NY : 81 + NY, :], (CORNER, 128)).astype(BF16)

    ids = jnp.transpose(wide[:, COLS : COLS + 128])[96:128]
    ids = jnp.concatenate([ids, ids], axis=1)
    modes = jnp.transpose(wide[:, COLS + 128 : COLS + 256])
    modes = jnp.concatenate([modes, modes], axis=1)
    port = lax.broadcasted_iota(jnp.int32, (PORTS, 2 * ROWS), 0).astype(F32)
    total = jnp.zeros((128, 128), F32)
    for tile in range(39):
        at = slice(tile * 128, (tile + 1) * 128)
        two_halves = [divmod(2 * tile, 3), divmod(2 * tile + 1, 3)]
        k0, k1 = two_halves[0][0], two_halves[1][0]
        r0 = jnp.broadcast_to(rate[:, k0 : k0 + 1], (ROWS, 128))
        if k1 != k0:
            r1 = jnp.broadcast_to(rate[:, k1 : k1 + 1], (ROWS, 128))
            r0 = jnp.where(low_rows, r0, r1)
        force[:, at] = -r0 * force[:, at]
        for x in range(NX):
            rows = slice(16 * x, 16 * x + NY)
            now = force[rows, at] + base_ref[x, :, at]
            force[rows, at] = now
            part_ref[x, :, at] = now
        high, low = split(force[:, at])
        picked = [
            jnp.where(ids[k : k + 1, :] == port, modes[32 * c + k : 32 * c + k + 1, :], 0.0)
            for k, c in two_halves
        ]
        left = jnp.concatenate(picked, axis=0).astype(BF16)
        total = total + bdot(left, jnp.concatenate([high, low], axis=0))
    rx_ref[:, :COLS] = force[80 : 80 + NY, :].astype(BF16)
    for x in range(NX):
        edge[x : x + 1, :COLS] = force[16 * x + NY : 16 * x + NY + 1, :]
    ry_ref[...] = edge[0:NX, 0:BACK].astype(BF16)
    rc_ref[:, :COLS] = jnp.broadcast_to(force[80 + NY : 81 + NY, :], (CORNER, COLS)).astype(BF16)
    amp[:, 0:64] = total[0:64, 0:64] + pltpu.roll(total[64:128, :], 64, 1)[:, 0:64]
    p_rows, p_cols = PORTS // n_y, 64 // n_x
    share_ref[...] = jnp.zeros((n_x * n_y, SHARE), F32)
    for q in range(p_rows):
        mine = amp[pl.ds(q, n_y, stride=p_rows), :] if p_rows > 1 else amp[...]
        for a in range(n_x):
            share_ref[a * n_y : (a + 1) * n_y, q * p_cols : (q + 1) * p_cols] = mine[
                :, a * p_cols : (a + 1) * p_cols
            ]


def last_kernel(part_ref, rx_ref, ry_ref, rc_ref, t_ref, d_ref):
    first = lax.broadcasted_iota(jnp.int32, (NY, BACK), 0) == 0
    for x in range(NX):
        row = ry_ref[x : x + 1, :].astype(F32)
        if x == 0:
            row = row + rc_ref[0:1, :].astype(F32)
        value = part_ref[x] + jnp.where(first, row, 0.0)
        if x == 0:
            value = value + rx_ref[...].astype(F32)
        t_ref[x] = value[:, :COLS].astype(BF16)
        d_ref[x] = value[:, COLS:]


def final_kernel(port_rows, port_cols, share_ref, d_ref, amp_ref, out_ref, lined):
    row = jnp.sum(share_ref[...], axis=0, keepdims=True)
    for q in range(port_rows):
        amp_ref[q : q + 1, :] = row[:, q * port_cols : (q + 1) * port_cols]
    for x in range(NX):
        for c in range(3):
            lined[x, :, c, :] = d_ref[x, :, 32 * c : 32 * c + NZ]
        out_ref[x] = lined[x].astype(BF16)


def per_device(
    disp,
    disp_prev,
    tangent,
    tangent_prev,
    lame_lambda,
    lame_mu,
    node_mass,
    force,
    cell_block,
    direction_block,
    port_id,
    port_mode,
):
    tab = tables()
    nx_dev, ny_dev = lax.axis_size("gx"), lax.axis_size("gy")
    vmem = pl.BlockSpec(memory_space=pltpu.VMEM)
    hbm = pl.BlockSpec(memory_space=pltpu.HBM)
    params = pltpu.CompilerParams(vmem_limit_bytes=VMEM_LIMIT)

    def step(shift_x, shift_y):
        route = []
        for i in range(nx_dev):
            for j in range(ny_dev):
                a, b = i + shift_x, j + shift_y
                if 0 <= a < nx_dev and 0 <= b < ny_dev:
                    route.append((i * ny_dev + j, a * ny_dev + b))
        return route

    def send(block, shift_x, shift_y):
        return lax.ppermute(block, ("gx", "gy"), step(shift_x, shift_y))

    by_comp = [a.transpose(0, 1, 3, 2) for a in (disp, port_mode, disp_prev, force)]
    raw = (tangent, by_comp[0], by_comp[1], node_mass, port_id, by_comp[2], by_comp[3])
    raw += (lame_lambda, lame_mu, cell_block, direction_block.reshape(1, 64))
    face_x, face_y, corner, small, own, par = pl.pallas_call(
        pack_kernel,
        out_shape=(
            jax.ShapeDtypeStruct((NY, WIDE), BF16),
            jax.ShapeDtypeStruct((NX, WIDE), BF16),
            jax.ShapeDtypeStruct((1, WIDE), BF16),
            jax.ShapeDtypeStruct((NX, NY, SMALL), BF16),
            jax.ShapeDtypeStruct((2, NX, NY, 128), F32),
            jax.ShapeDtypeStruct((24, 256), F32),
        ),
        in_specs=[hbm] * len(raw),
        out_specs=(vmem,) * 6,
        scratch_shapes=[
            pltpu.VMEM((NX, 16, SMALL), F32),
            pltpu.VMEM((8, WIDE), F32),
            pltpu.SemaphoreType.DMA((len(raw),)),
        ]
        + [pltpu.VMEM(a.shape, a.dtype) for a in raw],
        compiler_params=pltpu.CompilerParams(vmem_limit_bytes=VMEM_MOST),
    )(*raw)
    halo_x = send(face_x, -1, 0)
    halo_y = send(face_y, 0, -1)
    halo_c = send(corner, -1, -1)

    wide_table, short_table = (jnp.asarray(a) for a in tab)
    base, near, *near_tables = pl.pallas_call(
        local_kernel,
        out_shape=(
            jax.ShapeDtypeStruct((NX, NY, COLS), F32),
            jax.ShapeDtypeStruct((NX, NY, COLS), BF16),
            jax.ShapeDtypeStruct(wide_table.shape, F32),
            jax.ShapeDtypeStruct(short_table.shape, BF16),
        ),
        in_specs=[vmem] * 4,
        out_specs=(vmem,) * 4,
        compiler_params=params,
        cost_estimate=pl.CostEstimate(
            flops=4000000, bytes_accessed=8000000, transcendentals=0
        ),
    )(tangent, tangent_prev, wide_table, short_table)

    part, ret_x, ret_y, ret_c, shares = pl.pallas_call(
        functools.partial(main_kernel, nx_dev, ny_dev),
        out_shape=(
            jax.ShapeDtypeStruct((NX, NY, BACK), F32),
            jax.ShapeDtypeStruct((NY, BACK), BF16),
            jax.ShapeDtypeStruct((NX, BACK), BF16),
            jax.ShapeDtypeStruct((CORNER, BACK), BF16),
            jax.ShapeDtypeStruct((nx_dev * ny_dev, SHARE), F32),
        ),
        in_specs=[vmem] * 10,
        out_specs=(vmem,) * 5,
        scratch_shapes=[
            pltpu.VMEM((ROWS, WIDE), F32),
            pltpu.VMEM((2 * ROWS, 5 * 1152), BF16),
            pltpu.VMEM((3 * PTS, 1152), F32),
            pltpu.VMEM((256, 1152), F32),
            pltpu.VMEM((ROWS, COLS), F32),
            pltpu.VMEM((PTS, BACK), F32),
            pltpu.VMEM((PORTS, 64), F32),
        ],
        compiler_params=params,
        cost_estimate=pl.CostEstimate(
            flops=400000000, bytes_accessed=8000000, transcendentals=0
        ),
    )(
        par,
        near,
        base,
        own,
        small,
        halo_x,
        halo_y,
        halo_c,
        *near_tables,
    )

    port_rows, port_cols = PORTS // ny_dev, 64 // nx_dev
    shares = lax.all_to_all(shares, ("gx", "gy"), 0, 0)
    back_c = send(ret_c, 1, 1)
    back_y = send(ret_y, 0, 1)
    back_x = send(ret_x, 1, 0)

    tangent_next, disp_wide = pl.pallas_call(
        last_kernel,
        out_shape=(
            jax.ShapeDtypeStruct((NX, NY, COLS), BF16),
            jax.ShapeDtypeStruct((NX, NY, 128), F32),
        ),
        in_specs=[vmem] * 4,
        out_specs=(vmem, vmem),
        compiler_params=params,
        cost_estimate=pl.CostEstimate(flops=4000000, bytes_accessed=8000000, transcendentals=0),
    )(part, back_x, back_y, back_c)
    port_amp, disp_next = pl.pallas_call(
        functools.partial(final_kernel, port_rows, port_cols),
        out_shape=(
            jax.ShapeDtypeStruct((port_rows, port_cols), F32),
            jax.ShapeDtypeStruct((NX, NY, 3, NZ), BF16),
        ),
        in_specs=[vmem, vmem],
        out_specs=(vmem, vmem),
        scratch_shapes=[pltpu.VMEM((NX, NY, 3, NZ), F32)],
        compiler_params=params,
    )(shares, disp_wide)
    return (disp_next.transpose(0, 1, 3, 2), tangent_next, port_amp)


def solution(mesh):
    return jax.shard_map(
        per_device,
        mesh=mesh,
        in_specs=(
            P("gx", "gy", None, None),
            P("gx", "gy", None, None),
            P("gx", "gy", None),
            P("gx", "gy", None),
            P("gx", "gy", None),
            P("gx", "gy", None),
            P("gx", "gy", None),
            P("gx", "gy", None, None),
            P("gx", "gy", None),
            P(),
            P("gx", "gy", None),
            P("gx", "gy", None, None),
        ),
        out_specs=(P("gx", "gy", None, None), P("gx", "gy", None), P("gy", "gx")),
        check_vma=False,
    )
```

```python
import functools

import jax
import jax.numpy as jnp
import ml_dtypes
import numpy as np
from jax import lax
from jax.experimental import pallas as pl
from jax.experimental.pallas import tpu as pltpu
from jax.sharding import PartitionSpec as P

PORTS = 64
GLL_POINTS = np.array(
    [-1.0, -0.765055323929465, -0.285231516480645, 0.285231516480645, 0.765055323929465, 1.0]
)
GLL_WEIGHTS = np.array(
    [
        1.0 / 15.0,
        0.378474956297847,
        0.554858377035486,
        0.554858377035486,
        0.378474956297847,
        1.0 / 15.0,
    ]
)
STEP_SQUARED = 0.03
F32 = jnp.float32
BF16 = jnp.bfloat16

NX, NY, NZ = 5, 10, 26
COLS = 4992
SMALL = 384
WIDE = COLS + SMALL
BACK = COLS + 128
ROWS = 96
PTS = 72
VMEM_LIMIT = 24 * 1024 * 1024
VMEM_MOST = 60 * 1024 * 1024
UNROLL = 9
SHARE = 32


def derivative_table():
    identity = np.eye(6)
    differences = GLL_POINTS[:, None] - GLL_POINTS[None, :] + identity
    barycentric = 1.0 / np.prod(differences, axis=1)
    matrix = barycentric[None, :] / barycentric[:, None] / differences
    matrix = matrix * (1.0 - identity)
    matrix = matrix - identity * matrix.sum(axis=1)[:, None]
    return matrix


def halves(matrix):
    matrix = matrix.astype(np.float32)
    high = matrix.astype(ml_dtypes.bfloat16)
    low = (matrix - high.astype(np.float32)).astype(ml_dtypes.bfloat16)
    return high, low


SYM = {(0, 0): 0, (1, 1): 1, (2, 2): 2, (0, 1): 3, (0, 2): 4, (1, 2): 5}


def sym_of(c, d):
    return SYM[(min(c, d), max(c, d))]


@functools.cache
def tables():
    deriv = derivative_table()
    w = GLL_WEIGHTS
    fx = np.zeros((PTS, ROWS))
    fy = np.zeros((PTS, ROWS))
    fv = np.zeros((PTS, ROWS))
    wxy = np.zeros(PTS)
    for e in range(2):
        for px in range(6):
            for py in range(6):
                r = e * 36 + px * 6 + py
                wxy[r] = w[px] * w[py]
                fv[r, 16 * px + 5 * e + py] = 1.0
                for a in range(6):
                    fx[r, 16 * a + 5 * e + py] += deriv[px, a]
                    fy[r, 16 * px + 5 * e + a] += deriv[py, a]
    forward = np.concatenate([fx, fy, fv], axis=0)
    f_high, f_low = halves(forward)
    forward2 = np.concatenate([f_high, f_low], axis=1)
    backward = np.concatenate([(m * wxy[:, None]).T for m in (fx, fy, fv)], axis=1)
    b_high, b_low = halves(backward)
    backward2 = np.concatenate([b_high, b_low], axis=0)

    coef = np.zeros((2, 39, 128))
    for n in range(3):
        for m in range(3):
            a = np.repeat([deriv[2 * n, 2 * m], deriv[2 * n + 1, 2 * m + 1]], 64)
            b = np.repeat([deriv[2 * n, 2 * m + 1], deriv[2 * n + 1, 2 * m]], 64)
            at = np.repeat([deriv[2 * m, 2 * n], deriv[2 * m + 1, 2 * n + 1]], 64)
            bt = np.repeat([deriv[2 * m + 1, 2 * n], deriv[2 * m, 2 * n + 1]], 64)
            for q, v in enumerate((a, b, at, bt)):
                coef[0, q * 9 + n * 3 + m] = v
                coef[1, q * 9 + n * 3 + m] = np.roll(v, 64)
    for m in range(3):
        v = np.repeat([w[2 * m], w[2 * m + 1]], 64)
        coef[0, 36 + m] = v
        coef[1, 36 + m] = np.roll(v, 64)
    coef = np.repeat(coef.reshape(78, 1, 128), 8, axis=1).astype(np.float32)

    to_sym = np.zeros((3, 128, 512))
    from_sym = np.zeros((256, 384))
    merge = np.zeros((128, 128))
    for i in range(5):
        for kp in range(6):
            base = i * 36 + kp * 6
            for c in range(3):
                merge[i * 18 + c * 6 + kp, c * 32 + 5 * i + kp] = 1.0
                for d in range(3):
                    s = base + sym_of(c, d)
                    targets = [(s, 2.0 if c == d else 1.0)]
                    if c == d:
                        targets += [(256 + base + q, 1.0) for q in range(3)]
                    for column, factor in targets:
                        if d < 2:
                            to_sym[d, c * 32 + 5 * i + kp, column] += factor
                        else:
                            for k in range(6):
                                to_sym[2, c * 32 + 5 * i + k, column] += factor * deriv[kp, k]
                    if d < 2:
                        from_sym[s, d * 128 + i * 18 + c * 6 + kp] += w[kp]
                    else:
                        for k in range(6):
                            from_sym[s, 256 + i * 18 + c * 6 + k] += w[kp] * deriv[kp, k]
    spread = np.zeros((128, 128))
    for piece in range(3):
        for k in range(NZ):
            for c in range(3):
                spread[piece * 32 + k, c * 32 + k] = 1.0
    of_first = np.tile(np.arange(PTS) < 36, 3)[None, :]
    back_el = np.concatenate([backward * of_first, backward * ~of_first], axis=0)
    wide = np.zeros((952, 512), np.float32)
    wide[0:384] = to_sym.reshape(384, 512)
    wide[384:640, 0:384] = from_sym
    wide[384:512, 384:512] = merge
    wide[640:832, 0:216] = back_el
    wide[640:952, 256:384] = coef[0:39].reshape(312, 128)
    wide[640:952, 384:512] = coef[39:78].reshape(312, 128)
    short = np.zeros((544, 256), ml_dtypes.bfloat16)
    short[0:216, 0:192] = forward2
    short[224:416, 0:216] = backward2
    short[416:544, 0:128] = spread
    return wide, short


def fdot(a, b):
    (a_high, a_low), (b_high, b_low) = split(a), split(b)
    return bdot(a_high, b_high) + (bdot(a_low, b_high) + bdot(a_high, b_low))


def bdot(a, b):
    return jnp.dot(a, b, preferred_element_type=F32)


def split(value):
    high = value.astype(BF16)
    return high, (value - high.astype(F32)).astype(BF16)


def fetch(pairs, sem):
    copies = [pltpu.make_async_copy(src, dst, sem.at[n]) for n, (src, dst) in enumerate(pairs)]
    for copy in copies:
        copy.start()
    return copies


def pack_kernel(*refs):
    sources, (x_ref, y_ref, c_ref, s_ref, own_ref, par_ref) = refs[0:11], refs[11:17]
    small, wide, sem = refs[17:20]
    here = refs[20:]
    t_ref, d_ref, m_ref, mass_ref, id_ref, dp_ref, f_ref, lam_ref, mu_ref, cell_ref, dir_ref = here
    copies = fetch(zip(sources, here, strict=True), sem)
    small[...] = jnp.zeros((NX, 16, SMALL), F32)
    own_ref[...] = jnp.zeros((2, NX, NY, 128), F32)
    for copy in copies[1:]:
        copy.wait()
    for x in range(NX):
        d = d_ref[x].astype(F32)
        m = m_ref[x].astype(F32)
        before = 2.0 * d - dp_ref[x].astype(F32)
        f = f_ref[x].astype(F32)
        for c in range(3):
            small[x, 0:NY, 32 * c : 32 * c + NZ] = d[:, c, :]
            small[x, 0:NY, 128 + 32 * c : 128 + 32 * c + NZ] = m[:, c, :]
            own_ref[0, x, :, 32 * c : 32 * c + NZ] = before[:, c, :]
            own_ref[1, x, :, 32 * c : 32 * c + NZ] = f[:, c, :]
        small[x, 0:NY, 96 : 96 + NZ] = id_ref[x].astype(F32)
        rest = mass_ref[x]
        for piece in range(3):
            part = rest.astype(BF16).astype(F32)
            small[x, 0:NY, 256 + 32 * piece : 256 + 32 * piece + NZ] = part
            rest = rest - part
        s_ref[x] = small[x, 0:NY, :].astype(BF16)
    along_z = lax.broadcasted_iota(jnp.int32, (1, 256), 1) // 36
    for q, ref in enumerate((lam_ref, mu_ref)):
        values = ref[0].astype(F32)
        for e in range(2):
            row = jnp.zeros((1, 256), F32)
            for i in range(5):
                row = jnp.where(
                    along_z == i, jnp.broadcast_to(values[e : e + 1, i : i + 1], (1, 256)), row
                )
            par_ref[2 * q + e : 2 * q + e + 1, :] = row
    dirs = jnp.concatenate([dir_ref[...], dir_ref[...]], axis=1)
    cells = cell_ref[0]
    for e in range(2):
        for i in range(5):
            same = dirs == jnp.broadcast_to(cells[e : e + 1, i : i + 1], (1, 128))
            par_ref[8 + 5 * e + i : 9 + 5 * e + i, 0:128] = jnp.where(same, 1.0, 0.0)
    copies[0].wait()
    x_ref[:, :COLS] = t_ref[0]
    x_ref[:, COLS:] = small[0, 0:NY, :].astype(BF16)
    for x in range(NX):
        wide[x : x + 1, :COLS] = t_ref[x, 0:1, :].astype(F32)
        wide[x : x + 1, COLS:] = small[x, 0:1, :]
    y_ref[...] = wide[0:NX, :].astype(BF16)
    c_ref[...] = wide[0:1, :].astype(BF16)


def local_kernel(t_ref, tp_ref, wide_in, short_in, base_ref, copy_ref, wide_out, short_out):
    wide_out[...] = wide_in[...]
    short_out[...] = short_in[...]
    for x in range(NX):
        now = t_ref[x]
        copy_ref[x] = now
        base_ref[x] = 2.0 * now.astype(F32) - tp_ref[x].astype(F32)


def main_kernel(
    n_x,
    n_y,
    par_ref,
    t_ref,
    base_ref,
    own_ref,
    s_ref,
    hx_ref,
    hy_ref,
    hc_ref,
    *rest,
):
    tab, short = rest[0:2]
    part_ref, rx_ref, ry_ref, share_ref = rest[2:6]
    (wide, uc, grad, stress, force, edge, amp) = rest[6:]

    for x in range(NX):
        wide[16 * x + 8 : 16 * x + 16, :] = jnp.zeros((8, WIDE), F32)
        wide[16 * x : 16 * x + NY, :COLS] = t_ref[x].astype(F32)
        wide[16 * x : 16 * x + NY, COLS:] = s_ref[x].astype(F32)
        wide[16 * x + NY : 16 * x + NY + 1, :] = hy_ref[x : x + 1, :].astype(F32)
    wide[88:96, :] = jnp.zeros((8, WIDE), F32)
    wide[80 : 80 + NY, :] = hx_ref[...].astype(F32)
    wide[80 + NY : 81 + NY, :] = hc_ref[...].astype(F32)

    low_rows = lax.broadcasted_iota(jnp.int32, (ROWS, 128), 1) < 64
    first_el = lax.broadcasted_iota(jnp.int32, (PTS, 128), 0) < 36
    first_el2 = lax.broadcasted_iota(jnp.int32, (PTS, 256), 0) < 36

    for i in range(5):
        odd = i % 2
        tile0 = (960 * i - 64 * odd) // 128

        def source(index, tile0=tile0):
            return wide[:, (tile0 + index) * 128 : (tile0 + index + 1) * 128]

        for m in range(3):
            t = [source(3 * m + q) for q in range(3 + odd)]
            if odd:
                by_c = (
                    jnp.where(low_rows, t[2], t[0]),
                    pltpu.roll(jnp.where(low_rows, t[1], t[2]), 64, 1),
                    jnp.where(low_rows, t[3], t[1]),
                )
            else:
                by_c = (
                    jnp.where(low_rows, t[0], t[1]),
                    pltpu.roll(jnp.where(low_rows, t[2], t[0]), 64, 1),
                    jnp.where(low_rows, t[1], t[2]),
                )
            for c in range(3):
                at = i * 1152 + (c * 3 + m) * 128
                value = by_c[c].astype(BF16)
                uc[0:ROWS, at : at + 128] = value
                uc[ROWS : 2 * ROWS, at : at + 128] = value

    fwd = short[0:216, 0:192]
    bwd = short[224:416, :]

    small_nodes = wide[:, COLS : COLS + 128].astype(BF16)
    pg = bdot(fwd, jnp.concatenate([small_nodes, small_nodes], axis=0))
    both = fdot(pg[0:PTS], tab[0:128, :])
    both = both + fdot(pg[PTS : 2 * PTS], tab[128:256, :])
    both = both + fdot(pg[2 * PTS : 3 * PTS], tab[256:384, :])
    lam_l = jnp.where(first_el2, par_ref[0:1, :], par_ref[1:2, :])
    mu_l = jnp.where(first_el2, par_ref[2:3, :], par_ref[3:4, :])
    primal_stress = lam_l * both[:, 256:512] + mu_l * both[:, 0:256]
    unit = fdot(both[:, 0:256], tab[384:640, 0:384])
    full = fdot(primal_stress, tab[384:640, 0:384])
    terms = jnp.zeros((2 * ROWS, 256), F32)
    for d in range(3):
        pair = jnp.concatenate([a[:, d * 128 : (d + 1) * 128] for a in (unit, full)], axis=1)
        terms = terms + fdot(tab[640:832, d * PTS : (d + 1) * PTS], pair)
    unit_first, unit_second = terms[0:ROWS, 0:128], terms[ROWS : 2 * ROWS, 0:128]
    primal_force = fdot(terms[0:ROWS, 128:256] + terms[ROWS : 2 * ROWS, 128:256], tab[384:512, 384:512])

    force[...] = jnp.zeros((ROWS, COLS), F32)
    lane = lax.broadcasted_iota(jnp.int32, (ROWS, 128), 1)
    row40 = lax.broadcasted_iota(jnp.int32, (40, 128), 0)
    half40 = lax.broadcasted_iota(jnp.int32, (40, 128), 1) // 64

    for i in range(5):
        odd = i % 2
        grad[...] = bdot(fwd, uc[:, i * 1152 : (i + 1) * 1152])
        lam_rows, mu_rows = (
            jnp.where(
                first_el,
                *(
                    jnp.broadcast_to(par_ref[r : r + 1, 36 * i : 36 * i + 1], (PTS, 128))
                    for r in (q, q + 1)
                ),
            )
            for q in (0, 2)
        )
        edge[0:PTS, 0:128] = lam_rows
        edge[0:PTS, 128:256] = mu_rows
        pick = [par_ref[8 + 5 * e + i : 9 + 5 * e + i, 0:128] for e in range(2)]
        for c in range(3):
            for m in range(3):
                target = c * 6 + 2 * m + (1 - half40 if odd else half40)
                value = jnp.where(
                    row40 == target,
                    pick[0],
                    jnp.where(row40 == target + 18, pick[1], 0.0),
                )
                stress[216:256, (c * 3 + m) * 128 : (c * 3 + m + 1) * 128] = value

        def rows_step(rc, carry, odd=odd):
            row = pl.multiple_of(rc * 8, 8)

            def tile(kind, c, m):
                at = pl.multiple_of(kind * PTS + rc * 8, 8)
                return grad[pl.ds(at, 8), (c * 3 + m) * 128 : (c * 3 + m + 1) * 128]

            def coef(index):
                at = 256 + 128 * odd
                return tab[640 + 8 * index : 648 + 8 * index, at : at + 128]

            def put(direction, c, m, value):
                at = pl.multiple_of(direction * PTS + rc * 8, 8)
                stress[pl.ds(at, 8), (c * 3 + m) * 128 : (c * 3 + m + 1) * 128] = value

            def along_z(tiles, offset):
                turned = [pltpu.roll(v, 64, 1) for v in tiles]
                return [
                    sum(
                        coef(offset + n * 3 + m) * tiles[m]
                        + coef(offset + 9 + n * 3 + m) * turned[m]
                        for m in range(3)
                    )
                    for n in range(3)
                ]

            gz = [along_z([tile(2, c, m) for m in range(3)], 0) for c in range(3)]
            lam = edge[pl.ds(row, 8), 0:128]
            mu = edge[pl.ds(row, 8), 128:256]
            z_stress = [[None] * 3 for _ in range(3)]
            for m in range(3):
                wz = coef(36 + m)
                muw = mu * wz
                g = [[tile(0, c, m) for c in range(3)], [tile(1, c, m) for c in range(3)]]
                g.append([gz[c][m] for c in range(3)])
                dil = (lam * wz) * (g[0][0] + g[1][1] + g[2][2])
                put(0, 0, m, (muw + muw) * g[0][0] + dil)
                put(1, 1, m, (muw + muw) * g[1][1] + dil)
                z_stress[2][m] = (muw + muw) * g[2][2] + dil
                value = muw * (g[0][1] + g[1][0])
                put(0, 1, m, value)
                put(1, 0, m, value)
                value = muw * (g[0][2] + g[2][0])
                put(0, 2, m, value)
                z_stress[0][m] = value
                value = muw * (g[1][2] + g[2][1])
                put(1, 2, m, value)
                z_stress[1][m] = value
            for c in range(3):
                for n, value in enumerate(along_z(z_stress[c], 18)):
                    put(2, c, n, value)
            return carry

        lax.fori_loop(0, 9, rows_step, 0, unroll=UNROLL)
        s_high = stress[...].astype(BF16)
        s_low = (stress[0:216, :] - s_high[0:216].astype(F32)).astype(BF16)
        unit_here = jnp.where(
            lane < 106,
            pltpu.roll(unit_first, (88 - 18 * i) % 128, 1),
            pltpu.roll(unit_second, (106 - 18 * i) % 128, 1),
        )
        unit_high, unit_low = split(unit_here)
        unit_both = jnp.concatenate([unit_high, unit_low], axis=0)
        lane2 = lax.broadcasted_iota(jnp.int32, (2 * ROWS, 128), 1)
        inside = (lane2 >= 88) & (lane2 < 124)
        left = jnp.concatenate(
            [
                bwd[:, 0:128],
                jnp.where(inside, unit_both.astype(F32), bwd[:, 128:256].astype(F32)).astype(BF16),
            ],
            axis=1,
        )
        two = bdot(left, s_high)
        nodes = two[0:ROWS] + two[ROWS : 2 * ROWS] + bdot(bwd[0:ROWS, 0:216], s_low)

        def node_tile(c, m, nodes=nodes):
            return nodes[:, (c * 3 + m) * 128 : (c * 3 + m + 1) * 128]

        tile0 = (960 * i - 64 * odd) // 128

        def add(index, value, tile0=tile0):
            at = (tile0 + index) * 128
            force[:, at : at + 128] = force[:, at : at + 128] + value

        zero = jnp.zeros((ROWS, 128), F32)
        last_c2 = zero
        for m in range(3):
            c0, c2 = node_tile(0, m), node_tile(2, m)
            c1 = pltpu.roll(node_tile(1, m), 64, 1)
            if odd:
                add(3 * m, jnp.where(low_rows, last_c2, c0))
                add(3 * m + 1, jnp.where(low_rows, c1, c2))
                add(3 * m + 2, jnp.where(low_rows, c0, c1))
                last_c2 = c2
            else:
                add(3 * m, jnp.where(low_rows, c0, c1))
                add(3 * m + 1, jnp.where(low_rows, c2, c0))
                add(3 * m + 2, jnp.where(low_rows, c1, c2))
        if odd:
            add(9, jnp.where(low_rows, last_c2, zero))

    mass = bdot(wide[:, COLS + 256 : COLS + 384].astype(BF16), short[416:544, 0:128])
    rate = STEP_SQUARED / jnp.where(mass > 0.0, mass, 1.0)
    primal_step = -rate * primal_force
    for x in range(NX):
        part_ref[x, :, COLS:] = (
            primal_step[16 * x : 16 * x + NY, :]
            + own_ref[0, x]
            + rate[16 * x : 16 * x + NY, :] * own_ref[1, x]
        )
    rx_ref[:, COLS:] = primal_step[80 : 81 + NY, :].astype(BF16)
    for x in range(NX):
        edge[x : x + 1, COLS:BACK] = primal_step[16 * x + NY : 16 * x + NY + 1, :]

    ids = jnp.transpose(wide[:, COLS : COLS + 128])[96:128]
    ids = jnp.concatenate([ids, ids], axis=1)
    modes = jnp.transpose(wide[:, COLS + 128 : COLS + 256])
    modes = jnp.concatenate([modes, modes], axis=1)
    port = lax.broadcasted_iota(jnp.int32, (PORTS, 2 * ROWS), 0).astype(F32)
    total = jnp.zeros((128, 128), F32)
    for tile in range(39):
        at = slice(tile * 128, (tile + 1) * 128)
        two_halves = [divmod(2 * tile, 3), divmod(2 * tile + 1, 3)]
        k0, k1 = two_halves[0][0], two_halves[1][0]
        r0 = jnp.broadcast_to(rate[:, k0 : k0 + 1], (ROWS, 128))
        if k1 != k0:
            r1 = jnp.broadcast_to(rate[:, k1 : k1 + 1], (ROWS, 128))
            r0 = jnp.where(low_rows, r0, r1)
        force[:, at] = -r0 * force[:, at]
        for x in range(NX):
            rows = slice(16 * x, 16 * x + NY)
            now = force[rows, at] + base_ref[x, :, at]
            force[rows, at] = now
            part_ref[x, :, at] = now
        high, low = split(force[:, at])
        picked = [
            jnp.where(ids[k : k + 1, :] == port, modes[32 * c + k : 32 * c + k + 1, :], 0.0)
            for k, c in two_halves
        ]
        left = jnp.concatenate(picked, axis=0).astype(BF16)
        total = total + bdot(left, jnp.concatenate([high, low], axis=0))
    rx_ref[:, :COLS] = force[80 : 81 + NY, :].astype(BF16)
    for x in range(NX):
        edge[x : x + 1, :COLS] = force[16 * x + NY : 16 * x + NY + 1, :]
    ry_ref[...] = edge[0:NX, 0:BACK].astype(BF16)
    amp[:, 0:64] = total[0:64, 0:64] + pltpu.roll(total[64:128, :], 64, 1)[:, 0:64]
    p_rows, p_cols = PORTS // n_y, 64 // n_x
    share_ref[...] = jnp.zeros(share_ref.shape, F32)
    for q in range(p_rows):
        mine = amp[pl.ds(q, n_y, stride=p_rows), :] if p_rows > 1 else amp[...]
        for a in range(n_x):
            share_ref[a * n_y : (a + 1) * n_y, q * p_cols : (q + 1) * p_cols] = mine[
                :, a * p_cols : (a + 1) * p_cols
            ]


def relay_kernel(rx_ref, ry_ref, out_ref, rows):
    rows[0:NX, :] = ry_ref[...].astype(F32)
    rows[NX : NX + 1, :] = rx_ref[NY : NY + 1, :].astype(F32)
    out_ref[...] = rows[0 : NX + 1, :].astype(BF16)


def last_kernel(part_ref, rx_ref, ry_ref, t_ref, d_ref):
    first = lax.broadcasted_iota(jnp.int32, (NY, BACK), 0) == 0
    for x in range(NX):
        row = ry_ref[x : x + 1, :].astype(F32)
        if x == 0:
            row = row + ry_ref[NX : NX + 1, :].astype(F32)
        value = part_ref[x] + jnp.where(first, row, 0.0)
        if x == 0:
            value = value + rx_ref[0:NY, :].astype(F32)
        t_ref[x] = value[:, :COLS].astype(BF16)
        d_ref[x] = value[:, COLS:]


def final_kernel(port_rows, port_cols, share_ref, d_ref, amp_ref, out_ref, lined):
    row = jnp.sum(share_ref[...], axis=0, keepdims=True)
    for q in range(port_rows):
        amp_ref[q : q + 1, :] = row[:, q * port_cols : (q + 1) * port_cols]
    for x in range(NX):
        for c in range(3):
            lined[x, :, c, :] = d_ref[x, :, 32 * c : 32 * c + NZ]
        out_ref[x] = lined[x].astype(BF16)


def per_device(
    disp,
    disp_prev,
    tangent,
    tangent_prev,
    lame_lambda,
    lame_mu,
    node_mass,
    force,
    cell_block,
    direction_block,
    port_id,
    port_mode,
):
    tab = tables()
    share_lanes = max(SHARE, PORTS * 64 // (lax.axis_size("gx") * lax.axis_size("gy")))
    nx_dev, ny_dev = lax.axis_size("gx"), lax.axis_size("gy")
    vmem = pl.BlockSpec(memory_space=pltpu.VMEM)
    hbm = pl.BlockSpec(memory_space=pltpu.HBM)
    params = pltpu.CompilerParams(vmem_limit_bytes=VMEM_LIMIT)

    def step(shift_x, shift_y):
        route = []
        for i in range(nx_dev):
            for j in range(ny_dev):
                a, b = i + shift_x, j + shift_y
                if 0 <= a < nx_dev and 0 <= b < ny_dev:
                    route.append((i * ny_dev + j, a * ny_dev + b))
        return route

    def send(block, shift_x, shift_y):
        return lax.ppermute(block, ("gx", "gy"), step(shift_x, shift_y))

    by_comp = [a.transpose(0, 1, 3, 2) for a in (disp, port_mode, disp_prev, force)]
    raw = (tangent, by_comp[0], by_comp[1], node_mass, port_id, by_comp[2], by_comp[3])
    raw += (lame_lambda, lame_mu, cell_block, direction_block.reshape(1, 64))
    face_x, face_y, corner, small, own, par = pl.pallas_call(
        pack_kernel,
        out_shape=(
            jax.ShapeDtypeStruct((NY, WIDE), BF16),
            jax.ShapeDtypeStruct((NX, WIDE), BF16),
            jax.ShapeDtypeStruct((1, WIDE), BF16),
            jax.ShapeDtypeStruct((NX, NY, SMALL), BF16),
            jax.ShapeDtypeStruct((2, NX, NY, 128), F32),
            jax.ShapeDtypeStruct((24, 256), F32),
        ),
        in_specs=[hbm] * len(raw),
        out_specs=(vmem,) * 6,
        scratch_shapes=[
            pltpu.VMEM((NX, 16, SMALL), F32),
            pltpu.VMEM((8, WIDE), F32),
            pltpu.SemaphoreType.DMA((len(raw),)),
        ]
        + [pltpu.VMEM(a.shape, a.dtype) for a in raw],
        compiler_params=pltpu.CompilerParams(vmem_limit_bytes=VMEM_MOST),
    )(*raw)
    halo_x = send(face_x, -1, 0)
    halo_y = send(face_y, 0, -1)
    halo_c = send(corner, -1, -1)

    wide_table, short_table = (jnp.asarray(a) for a in tab)
    base, near, *near_tables = pl.pallas_call(
        local_kernel,
        out_shape=(
            jax.ShapeDtypeStruct((NX, NY, COLS), F32),
            jax.ShapeDtypeStruct((NX, NY, COLS), BF16),
            jax.ShapeDtypeStruct(wide_table.shape, F32),
            jax.ShapeDtypeStruct(short_table.shape, BF16),
        ),
        in_specs=[vmem] * 4,
        out_specs=(vmem,) * 4,
        compiler_params=params,
        cost_estimate=pl.CostEstimate(
            flops=4000000, bytes_accessed=8000000, transcendentals=0
        ),
    )(tangent, tangent_prev, wide_table, short_table)

    part, ret_x, ret_y, shares = pl.pallas_call(
        functools.partial(main_kernel, nx_dev, ny_dev),
        out_shape=(
            jax.ShapeDtypeStruct((NX, NY, BACK), F32),
            jax.ShapeDtypeStruct((NY + 1, BACK), BF16),
            jax.ShapeDtypeStruct((NX, BACK), BF16),
            jax.ShapeDtypeStruct((nx_dev * ny_dev, share_lanes), F32),
        ),
        in_specs=[vmem] * 10,
        out_specs=(vmem,) * 4,
        scratch_shapes=[
            pltpu.VMEM((ROWS, WIDE), F32),
            pltpu.VMEM((2 * ROWS, 5 * 1152), BF16),
            pltpu.VMEM((3 * PTS, 1152), F32),
            pltpu.VMEM((256, 1152), F32),
            pltpu.VMEM((ROWS, COLS), F32),
            pltpu.VMEM((PTS, BACK), F32),
            pltpu.VMEM((PORTS, 64), F32),
        ],
        compiler_params=params,
        cost_estimate=pl.CostEstimate(
            flops=400000000, bytes_accessed=8000000, transcendentals=0
        ),
    )(
        par,
        near,
        base,
        own,
        small,
        halo_x,
        halo_y,
        halo_c,
        *near_tables,
    )

    port_rows, port_cols = PORTS // ny_dev, 64 // nx_dev
    shares = lax.all_to_all(shares, ("gx", "gy"), 0, 0)
    back_x = send(ret_x, 1, 0)
    onward = pl.pallas_call(
        relay_kernel,
        out_shape=jax.ShapeDtypeStruct((NX + 1, BACK), BF16),
        in_specs=[vmem, vmem],
        out_specs=vmem,
        scratch_shapes=[pltpu.VMEM((8, BACK), F32)],
        compiler_params=params,
        cost_estimate=pl.CostEstimate(flops=100000, bytes_accessed=200000, transcendentals=0),
    )(back_x, ret_y)
    back_y = send(onward, 0, 1)

    tangent_next, disp_wide = pl.pallas_call(
        last_kernel,
        out_shape=(
            jax.ShapeDtypeStruct((NX, NY, COLS), BF16),
            jax.ShapeDtypeStruct((NX, NY, 128), F32),
        ),
        in_specs=[vmem] * 3,
        out_specs=(vmem, vmem),
        compiler_params=params,
        cost_estimate=pl.CostEstimate(flops=4000000, bytes_accessed=8000000, transcendentals=0),
    )(part, back_x, back_y)
    port_amp, disp_next = pl.pallas_call(
        functools.partial(final_kernel, port_rows, port_cols),
        out_shape=(
            jax.ShapeDtypeStruct((port_rows, port_cols), F32),
            jax.ShapeDtypeStruct((NX, NY, 3, NZ), BF16),
        ),
        in_specs=[vmem, vmem],
        out_specs=(vmem, vmem),
        scratch_shapes=[pltpu.VMEM((NX, NY, 3, NZ), F32)],
        compiler_params=params,
    )(shares, disp_wide)
    return (disp_next.transpose(0, 1, 3, 2), tangent_next, port_amp)


def solution(mesh):
    return jax.shard_map(
        per_device,
        mesh=mesh,
        in_specs=(
            P("gx", "gy", None, None),
            P("gx", "gy", None, None),
            P("gx", "gy", None),
            P("gx", "gy", None),
            P("gx", "gy", None),
            P("gx", "gy", None),
            P("gx", "gy", None),
            P("gx", "gy", None, None),
            P("gx", "gy", None),
            P(),
            P("gx", "gy", None),
            P("gx", "gy", None, None),
        ),
        out_specs=(P("gx", "gy", None, None), P("gx", "gy", None), P("gy", "gx")),
        check_vma=False,
    )
```

```python
import functools

import jax
import jax.numpy as jnp
import ml_dtypes
import numpy as np
from jax import lax
from jax.experimental import pallas as pl
from jax.experimental.pallas import tpu as pltpu
from jax.sharding import PartitionSpec as P

PORTS = 64
GLL_POINTS = np.array(
    [-1.0, -0.765055323929465, -0.285231516480645, 0.285231516480645, 0.765055323929465, 1.0]
)
GLL_WEIGHTS = np.array(
    [
        1.0 / 15.0,
        0.378474956297847,
        0.554858377035486,
        0.554858377035486,
        0.378474956297847,
        1.0 / 15.0,
    ]
)
STEP_SQUARED = 0.03
F32 = jnp.float32
BF16 = jnp.bfloat16

NX, NY, NZ = 5, 10, 26
COLS = 4992
SMALL = 384
WIDE = COLS + SMALL
BACK = COLS + 128
ROWS = 96
PTS = 72
VMEM_LIMIT = 24 * 1024 * 1024
VMEM_MOST = 60 * 1024 * 1024
UNROLL = 9
SHARE = 32


def derivative_table():
    identity = np.eye(6)
    differences = GLL_POINTS[:, None] - GLL_POINTS[None, :] + identity
    barycentric = 1.0 / np.prod(differences, axis=1)
    matrix = barycentric[None, :] / barycentric[:, None] / differences
    matrix = matrix * (1.0 - identity)
    matrix = matrix - identity * matrix.sum(axis=1)[:, None]
    return matrix


def halves(matrix):
    matrix = matrix.astype(np.float32)
    high = matrix.astype(ml_dtypes.bfloat16)
    low = (matrix - high.astype(np.float32)).astype(ml_dtypes.bfloat16)
    return high, low


SYM = {(0, 0): 0, (1, 1): 1, (2, 2): 2, (0, 1): 3, (0, 2): 4, (1, 2): 5}


def sym_of(c, d):
    return SYM[(min(c, d), max(c, d))]


@functools.cache
def tables():
    deriv = derivative_table()
    w = GLL_WEIGHTS
    fx = np.zeros((PTS, ROWS))
    fy = np.zeros((PTS, ROWS))
    fv = np.zeros((PTS, ROWS))
    wxy = np.zeros(PTS)
    for e in range(2):
        for px in range(6):
            for py in range(6):
                r = e * 36 + px * 6 + py
                wxy[r] = w[px] * w[py]
                fv[r, 16 * px + 5 * e + py] = 1.0
                for a in range(6):
                    fx[r, 16 * a + 5 * e + py] += deriv[px, a]
                    fy[r, 16 * px + 5 * e + a] += deriv[py, a]
    forward = np.concatenate([fx, fy, fv], axis=0)
    f_high, f_low = halves(forward)
    forward2 = np.concatenate([f_high, f_low], axis=1)
    backward = np.concatenate([(m * wxy[:, None]).T for m in (fx, fy, fv)], axis=1)
    b_high, b_low = halves(backward)
    backward2 = np.concatenate([b_high, b_low], axis=0)

    coef = np.zeros((2, 39, 128))
    for n in range(3):
        for m in range(3):
            a = np.repeat([deriv[2 * n, 2 * m], deriv[2 * n + 1, 2 * m + 1]], 64)
            b = np.repeat([deriv[2 * n, 2 * m + 1], deriv[2 * n + 1, 2 * m]], 64)
            at = np.repeat([deriv[2 * m, 2 * n], deriv[2 * m + 1, 2 * n + 1]], 64)
            bt = np.repeat([deriv[2 * m + 1, 2 * n], deriv[2 * m, 2 * n + 1]], 64)
            for q, v in enumerate((a, b, at, bt)):
                coef[0, q * 9 + n * 3 + m] = v
                coef[1, q * 9 + n * 3 + m] = np.roll(v, 64)
    for m in range(3):
        v = np.repeat([w[2 * m], w[2 * m + 1]], 64)
        coef[0, 36 + m] = v
        coef[1, 36 + m] = np.roll(v, 64)
    coef = np.repeat(coef.reshape(78, 1, 128), 8, axis=1).astype(np.float32)

    to_sym = np.zeros((3, 128, 512))
    from_sym = np.zeros((256, 384))
    merge = np.zeros((128, 128))
    for i in range(5):
        for kp in range(6):
            base = i * 36 + kp * 6
            for c in range(3):
                merge[i * 18 + c * 6 + kp, c * 32 + 5 * i + kp] = 1.0
                for d in range(3):
                    s = base + sym_of(c, d)
                    targets = [(s, 2.0 if c == d else 1.0)]
                    if c == d:
                        targets += [(256 + base + q, 1.0) for q in range(3)]
                    for column, factor in targets:
                        if d < 2:
                            to_sym[d, c * 32 + 5 * i + kp, column] += factor
                        else:
                            for k in range(6):
                                to_sym[2, c * 32 + 5 * i + k, column] += factor * deriv[kp, k]
                    if d < 2:
                        from_sym[s, d * 128 + i * 18 + c * 6 + kp] += w[kp]
                    else:
                        for k in range(6):
                            from_sym[s, 256 + i * 18 + c * 6 + k] += w[kp] * deriv[kp, k]
    spread = np.zeros((128, 128))
    for piece in range(3):
        for k in range(NZ):
            for c in range(3):
                spread[piece * 32 + k, c * 32 + k] = 1.0
    of_first = np.tile(np.arange(PTS) < 36, 3)[None, :]
    back_el = np.concatenate([backward * of_first, backward * ~of_first], axis=0)
    wide = np.zeros((952, 512), np.float32)
    wide[0:384] = to_sym.reshape(384, 512)
    wide[384:640, 0:384] = from_sym
    wide[384:512, 384:512] = merge
    wide[640:832, 0:216] = back_el
    wide[640:952, 256:384] = coef[0:39].reshape(312, 128)
    wide[640:952, 384:512] = coef[39:78].reshape(312, 128)
    short = np.zeros((544, 256), ml_dtypes.bfloat16)
    short[0:216, 0:192] = forward2
    short[224:416, 0:216] = backward2
    short[416:544, 0:128] = spread
    return wide, short


def fdot(a, b):
    (a_high, a_low), (b_high, b_low) = split(a), split(b)
    return bdot(a_high, b_high) + (bdot(a_low, b_high) + bdot(a_high, b_low))


def bdot(a, b):
    return jnp.dot(a, b, preferred_element_type=F32)


def split(value):
    high = value.astype(BF16)
    return high, (value - high.astype(F32)).astype(BF16)


def fetch(pairs, sem):
    copies = [pltpu.make_async_copy(src, dst, sem.at[n]) for n, (src, dst) in enumerate(pairs)]
    for copy in copies:
        copy.start()
    return copies


def pack_kernel(*refs):
    sources, (x_ref, y_ref, c_ref, s_ref, own_ref, par_ref) = refs[0:11], refs[11:17]
    small, wide, sem = refs[17:20]
    here = refs[20:]
    t_ref, d_ref, m_ref, mass_ref, id_ref, dp_ref, f_ref, lam_ref, mu_ref, cell_ref, dir_ref = here
    copies = fetch(zip(sources, here, strict=True), sem)
    small[...] = jnp.zeros((NX, 16, SMALL), F32)
    own_ref[...] = jnp.zeros((2, NX, NY, 128), F32)
    for copy in copies[1:]:
        copy.wait()
    for x in range(NX):
        d = d_ref[x].astype(F32)
        m = m_ref[x].astype(F32)
        before = 2.0 * d - dp_ref[x].astype(F32)
        f = f_ref[x].astype(F32)
        for c in range(3):
            small[x, 0:NY, 32 * c : 32 * c + NZ] = d[:, c, :]
            small[x, 0:NY, 128 + 32 * c : 128 + 32 * c + NZ] = m[:, c, :]
            own_ref[0, x, :, 32 * c : 32 * c + NZ] = before[:, c, :]
            own_ref[1, x, :, 32 * c : 32 * c + NZ] = f[:, c, :]
        small[x, 0:NY, 96 : 96 + NZ] = id_ref[x].astype(F32)
        rest = mass_ref[x]
        for piece in range(3):
            part = rest.astype(BF16).astype(F32)
            small[x, 0:NY, 256 + 32 * piece : 256 + 32 * piece + NZ] = part
            rest = rest - part
        s_ref[x] = small[x, 0:NY, :].astype(BF16)
    along_z = lax.broadcasted_iota(jnp.int32, (1, 256), 1) // 36
    for q, ref in enumerate((lam_ref, mu_ref)):
        values = ref[0].astype(F32)
        for e in range(2):
            row = jnp.zeros((1, 256), F32)
            for i in range(5):
                row = jnp.where(
                    along_z == i, jnp.broadcast_to(values[e : e + 1, i : i + 1], (1, 256)), row
                )
            par_ref[2 * q + e : 2 * q + e + 1, :] = row
    dirs = jnp.concatenate([dir_ref[...], dir_ref[...]], axis=1)
    cells = cell_ref[0]
    for e in range(2):
        for i in range(5):
            same = dirs == jnp.broadcast_to(cells[e : e + 1, i : i + 1], (1, 128))
            par_ref[8 + 5 * e + i : 9 + 5 * e + i, 0:128] = jnp.where(same, 1.0, 0.0)
    copies[0].wait()
    x_ref[:, :COLS] = t_ref[0]
    x_ref[:, COLS:] = small[0, 0:NY, :].astype(BF16)
    for x in range(NX):
        wide[x : x + 1, :COLS] = t_ref[x, 0:1, :].astype(F32)
        wide[x : x + 1, COLS:] = small[x, 0:1, :]
    y_ref[...] = wide[0:NX, :].astype(BF16)
    c_ref[...] = wide[0:1, :].astype(BF16)


def local_kernel(wide_in, short_in, wide_out, short_out):
    wide_out[...] = wide_in[...]
    short_out[...] = short_in[...]


def main_kernel(
    n_x,
    n_y,
    par_ref,
    t_ref,
    tp_ref,
    own_ref,
    s_ref,
    hx_ref,
    hy_ref,
    hc_ref,
    *rest,
):
    tab, short = rest[0:2]
    part_ref, rx_ref, ry_ref, share_ref = rest[2:6]
    (wide, uc, grad, stress, force, edge, amp) = rest[6:]

    for x in range(NX):
        wide[16 * x + 8 : 16 * x + 16, :] = jnp.zeros((8, WIDE), F32)
        wide[16 * x : 16 * x + NY, :COLS] = t_ref[x].astype(F32)
        wide[16 * x : 16 * x + NY, COLS:] = s_ref[x].astype(F32)
        wide[16 * x + NY : 16 * x + NY + 1, :] = hy_ref[x : x + 1, :].astype(F32)
    wide[88:96, :] = jnp.zeros((8, WIDE), F32)
    wide[80 : 80 + NY, :] = hx_ref[...].astype(F32)
    wide[80 + NY : 81 + NY, :] = hc_ref[...].astype(F32)

    low_rows = lax.broadcasted_iota(jnp.int32, (ROWS, 128), 1) < 64
    first_el = lax.broadcasted_iota(jnp.int32, (PTS, 128), 0) < 36
    first_el2 = lax.broadcasted_iota(jnp.int32, (PTS, 256), 0) < 36

    for i in range(5):
        odd = i % 2
        tile0 = (960 * i - 64 * odd) // 128

        def source(index, tile0=tile0):
            return wide[:, (tile0 + index) * 128 : (tile0 + index + 1) * 128]

        for m in range(3):
            t = [source(3 * m + q) for q in range(3 + odd)]
            if odd:
                by_c = (
                    jnp.where(low_rows, t[2], t[0]),
                    pltpu.roll(jnp.where(low_rows, t[1], t[2]), 64, 1),
                    jnp.where(low_rows, t[3], t[1]),
                )
            else:
                by_c = (
                    jnp.where(low_rows, t[0], t[1]),
                    pltpu.roll(jnp.where(low_rows, t[2], t[0]), 64, 1),
                    jnp.where(low_rows, t[1], t[2]),
                )
            for c in range(3):
                at = i * 1152 + (c * 3 + m) * 128
                value = by_c[c].astype(BF16)
                uc[0:ROWS, at : at + 128] = value
                uc[ROWS : 2 * ROWS, at : at + 128] = value

    fwd = short[0:216, 0:192]
    bwd = short[224:416, :]

    small_nodes = wide[:, COLS : COLS + 128].astype(BF16)
    pg = bdot(fwd, jnp.concatenate([small_nodes, small_nodes], axis=0))
    both = fdot(pg[0:PTS], tab[0:128, :])
    both = both + fdot(pg[PTS : 2 * PTS], tab[128:256, :])
    both = both + fdot(pg[2 * PTS : 3 * PTS], tab[256:384, :])
    lam_l = jnp.where(first_el2, par_ref[0:1, :], par_ref[1:2, :])
    mu_l = jnp.where(first_el2, par_ref[2:3, :], par_ref[3:4, :])
    primal_stress = lam_l * both[:, 256:512] + mu_l * both[:, 0:256]
    unit = fdot(both[:, 0:256], tab[384:640, 0:384])
    full = fdot(primal_stress, tab[384:640, 0:384])
    terms = jnp.zeros((2 * ROWS, 256), F32)
    for d in range(3):
        pair = jnp.concatenate([a[:, d * 128 : (d + 1) * 128] for a in (unit, full)], axis=1)
        terms = terms + fdot(tab[640:832, d * PTS : (d + 1) * PTS], pair)
    unit_first, unit_second = terms[0:ROWS, 0:128], terms[ROWS : 2 * ROWS, 0:128]
    primal_force = fdot(terms[0:ROWS, 128:256] + terms[ROWS : 2 * ROWS, 128:256], tab[384:512, 384:512])

    force[...] = jnp.zeros((ROWS, COLS), F32)
    grad[...] = bdot(fwd, uc[...])
    lane = lax.broadcasted_iota(jnp.int32, (ROWS, 128), 1)
    row40 = lax.broadcasted_iota(jnp.int32, (40, 128), 0)
    half40 = lax.broadcasted_iota(jnp.int32, (40, 128), 1) // 64

    for i in range(5):
        odd = i % 2
        lam_rows, mu_rows = (
            jnp.where(
                first_el,
                *(
                    jnp.broadcast_to(par_ref[r : r + 1, 36 * i : 36 * i + 1], (PTS, 128))
                    for r in (q, q + 1)
                ),
            )
            for q in (0, 2)
        )
        edge[0:PTS, 0:128] = lam_rows
        edge[0:PTS, 128:256] = mu_rows
        pick = [par_ref[8 + 5 * e + i : 9 + 5 * e + i, 0:128] for e in range(2)]
        for c in range(3):
            for m in range(3):
                target = c * 6 + 2 * m + (1 - half40 if odd else half40)
                value = jnp.where(
                    row40 == target,
                    pick[0],
                    jnp.where(row40 == target + 18, pick[1], 0.0),
                )
                stress[i, 216:256, (c * 3 + m) * 128 : (c * 3 + m + 1) * 128] = value

        def rows_step(rc, carry, odd=odd, i=i):
            row = pl.multiple_of(rc * 8, 8)

            def tile(kind, c, m):
                at = pl.multiple_of(kind * PTS + rc * 8, 8)
                lanes = i * 1152 + (c * 3 + m) * 128
                return grad[pl.ds(at, 8), lanes : lanes + 128]

            def coef(index):
                at = 256 + 128 * odd
                return tab[640 + 8 * index : 648 + 8 * index, at : at + 128]

            def put(direction, c, m, value):
                at = pl.multiple_of(direction * PTS + rc * 8, 8)
                stress[i, pl.ds(at, 8), (c * 3 + m) * 128 : (c * 3 + m + 1) * 128] = value

            def along_z(tiles, offset):
                turned = [pltpu.roll(v, 64, 1) for v in tiles]
                return [
                    sum(
                        coef(offset + n * 3 + m) * tiles[m]
                        + coef(offset + 9 + n * 3 + m) * turned[m]
                        for m in range(3)
                    )
                    for n in range(3)
                ]

            gz = [along_z([tile(2, c, m) for m in range(3)], 0) for c in range(3)]
            lam = edge[pl.ds(row, 8), 0:128]
            mu = edge[pl.ds(row, 8), 128:256]
            z_stress = [[None] * 3 for _ in range(3)]
            for m in range(3):
                wz = coef(36 + m)
                muw = mu * wz
                g = [[tile(0, c, m) for c in range(3)], [tile(1, c, m) for c in range(3)]]
                g.append([gz[c][m] for c in range(3)])
                dil = (lam * wz) * (g[0][0] + g[1][1] + g[2][2])
                put(0, 0, m, (muw + muw) * g[0][0] + dil)
                put(1, 1, m, (muw + muw) * g[1][1] + dil)
                z_stress[2][m] = (muw + muw) * g[2][2] + dil
                value = muw * (g[0][1] + g[1][0])
                put(0, 1, m, value)
                put(1, 0, m, value)
                value = muw * (g[0][2] + g[2][0])
                put(0, 2, m, value)
                z_stress[0][m] = value
                value = muw * (g[1][2] + g[2][1])
                put(1, 2, m, value)
                z_stress[1][m] = value
            for c in range(3):
                for n, value in enumerate(along_z(z_stress[c], 18)):
                    put(2, c, n, value)
            return carry

        lax.fori_loop(0, 9, rows_step, 0, unroll=UNROLL)
        s_high = stress[i].astype(BF16)
        s_low = (stress[i, 0:216, :] - s_high[0:216].astype(F32)).astype(BF16)
        unit_here = jnp.where(
            lane < 106,
            pltpu.roll(unit_first, (88 - 18 * i) % 128, 1),
            pltpu.roll(unit_second, (106 - 18 * i) % 128, 1),
        )
        unit_high, unit_low = split(unit_here)
        unit_both = jnp.concatenate([unit_high, unit_low], axis=0)
        lane2 = lax.broadcasted_iota(jnp.int32, (2 * ROWS, 128), 1)
        inside = (lane2 >= 88) & (lane2 < 124)
        left = jnp.concatenate(
            [
                bwd[:, 0:128],
                jnp.where(inside, unit_both.astype(F32), bwd[:, 128:256].astype(F32)).astype(BF16),
            ],
            axis=1,
        )
        two = bdot(left, s_high)
        nodes = two[0:ROWS] + two[ROWS : 2 * ROWS] + bdot(bwd[0:ROWS, 0:216], s_low)

        def node_tile(c, m, nodes=nodes):
            return nodes[:, (c * 3 + m) * 128 : (c * 3 + m + 1) * 128]

        tile0 = (960 * i - 64 * odd) // 128

        def add(index, value, tile0=tile0):
            at = (tile0 + index) * 128
            force[:, at : at + 128] = force[:, at : at + 128] + value

        zero = jnp.zeros((ROWS, 128), F32)
        last_c2 = zero
        for m in range(3):
            c0, c2 = node_tile(0, m), node_tile(2, m)
            c1 = pltpu.roll(node_tile(1, m), 64, 1)
            if odd:
                add(3 * m, jnp.where(low_rows, last_c2, c0))
                add(3 * m + 1, jnp.where(low_rows, c1, c2))
                add(3 * m + 2, jnp.where(low_rows, c0, c1))
                last_c2 = c2
            else:
                add(3 * m, jnp.where(low_rows, c0, c1))
                add(3 * m + 1, jnp.where(low_rows, c2, c0))
                add(3 * m + 2, jnp.where(low_rows, c1, c2))
        if odd:
            add(9, jnp.where(low_rows, last_c2, zero))

    mass = bdot(wide[:, COLS + 256 : COLS + 384].astype(BF16), short[416:544, 0:128])
    rate = STEP_SQUARED / jnp.where(mass > 0.0, mass, 1.0)
    primal_step = -rate * primal_force
    for x in range(NX):
        part_ref[x, :, COLS:] = (
            primal_step[16 * x : 16 * x + NY, :]
            + own_ref[0, x]
            + rate[16 * x : 16 * x + NY, :] * own_ref[1, x]
        )
    rx_ref[:, COLS:] = primal_step[80 : 81 + NY, :].astype(BF16)
    for x in range(NX):
        edge[x : x + 1, COLS:BACK] = primal_step[16 * x + NY : 16 * x + NY + 1, :]

    ids = jnp.transpose(wide[:, COLS : COLS + 128])[96:128]
    ids = jnp.concatenate([ids, ids], axis=1)
    modes = jnp.transpose(wide[:, COLS + 128 : COLS + 256])
    modes = jnp.concatenate([modes, modes], axis=1)
    port = lax.broadcasted_iota(jnp.int32, (PORTS, 2 * ROWS), 0).astype(F32)
    total = jnp.zeros((128, 128), F32)
    for tile in range(39):
        at = slice(tile * 128, (tile + 1) * 128)
        two_halves = [divmod(2 * tile, 3), divmod(2 * tile + 1, 3)]
        k0, k1 = two_halves[0][0], two_halves[1][0]
        r0 = jnp.broadcast_to(rate[:, k0 : k0 + 1], (ROWS, 128))
        if k1 != k0:
            r1 = jnp.broadcast_to(rate[:, k1 : k1 + 1], (ROWS, 128))
            r0 = jnp.where(low_rows, r0, r1)
        force[:, at] = -r0 * force[:, at]
        for x in range(NX):
            rows = slice(16 * x, 16 * x + NY)
            now = force[rows, at] + 2.0 * wide[rows, at] - tp_ref[x, :, at].astype(F32)
            force[rows, at] = now
            part_ref[x, :, at] = now
        high, low = split(force[:, at])
        picked = [
            jnp.where(ids[k : k + 1, :] == port, modes[32 * c + k : 32 * c + k + 1, :], 0.0)
            for k, c in two_halves
        ]
        left = jnp.concatenate(picked, axis=0).astype(BF16)
        total = total + bdot(left, jnp.concatenate([high, low], axis=0))
    rx_ref[:, :COLS] = force[80 : 81 + NY, :].astype(BF16)
    for x in range(NX):
        edge[x : x + 1, :COLS] = force[16 * x + NY : 16 * x + NY + 1, :]
    ry_ref[...] = edge[0:NX, 0:BACK].astype(BF16)
    amp[:, 0:64] = total[0:64, 0:64] + pltpu.roll(total[64:128, :], 64, 1)[:, 0:64]
    p_rows, p_cols = PORTS // n_y, 64 // n_x
    share_ref[...] = jnp.zeros(share_ref.shape, F32)
    for q in range(p_rows):
        mine = amp[pl.ds(q, n_y, stride=p_rows), :] if p_rows > 1 else amp[...]
        for a in range(n_x):
            share_ref[a * n_y : (a + 1) * n_y, q * p_cols : (q + 1) * p_cols] = mine[
                :, a * p_cols : (a + 1) * p_cols
            ]


def relay_kernel(rx_ref, ry_ref, out_ref, rows):
    rows[0:NX, :] = ry_ref[...].astype(F32)
    rows[NX : NX + 1, :] = rx_ref[NY : NY + 1, :].astype(F32)
    out_ref[...] = rows[0 : NX + 1, :].astype(BF16)


def last_kernel(part_ref, rx_ref, ry_ref, t_ref, d_ref):
    first = lax.broadcasted_iota(jnp.int32, (NY, BACK), 0) == 0
    for x in range(NX):
        row = ry_ref[x : x + 1, :].astype(F32)
        if x == 0:
            row = row + ry_ref[NX : NX + 1, :].astype(F32)
        value = part_ref[x] + jnp.where(first, row, 0.0)
        if x == 0:
            value = value + rx_ref[0:NY, :].astype(F32)
        t_ref[x] = value[:, :COLS].astype(BF16)
        d_ref[x] = value[:, COLS:]


def final_kernel(port_rows, port_cols, share_ref, d_ref, amp_ref, out_ref, lined):
    row = jnp.sum(share_ref[...], axis=0, keepdims=True)
    for q in range(port_rows):
        amp_ref[q : q + 1, :] = row[:, q * port_cols : (q + 1) * port_cols]
    for x in range(NX):
        for c in range(3):
            lined[x, :, c, :] = d_ref[x, :, 32 * c : 32 * c + NZ]
        out_ref[x] = lined[x].astype(BF16)


def per_device(
    disp,
    disp_prev,
    tangent,
    tangent_prev,
    lame_lambda,
    lame_mu,
    node_mass,
    force,
    cell_block,
    direction_block,
    port_id,
    port_mode,
):
    tab = tables()
    share_lanes = max(SHARE, PORTS * 64 // (lax.axis_size("gx") * lax.axis_size("gy")))
    nx_dev, ny_dev = lax.axis_size("gx"), lax.axis_size("gy")
    vmem = pl.BlockSpec(memory_space=pltpu.VMEM)
    hbm = pl.BlockSpec(memory_space=pltpu.HBM)
    params = pltpu.CompilerParams(vmem_limit_bytes=VMEM_LIMIT)

    def step(shift_x, shift_y):
        route = []
        for i in range(nx_dev):
            for j in range(ny_dev):
                a, b = i + shift_x, j + shift_y
                if 0 <= a < nx_dev and 0 <= b < ny_dev:
                    route.append((i * ny_dev + j, a * ny_dev + b))
        return route

    def send(block, shift_x, shift_y):
        return lax.ppermute(block, ("gx", "gy"), step(shift_x, shift_y))

    by_comp = [a.transpose(0, 1, 3, 2) for a in (disp, port_mode, disp_prev, force)]
    raw = (tangent, by_comp[0], by_comp[1], node_mass, port_id, by_comp[2], by_comp[3])
    raw += (lame_lambda, lame_mu, cell_block, direction_block.reshape(1, 64))
    face_x, face_y, corner, small, own, par = pl.pallas_call(
        pack_kernel,
        out_shape=(
            jax.ShapeDtypeStruct((NY, WIDE), BF16),
            jax.ShapeDtypeStruct((NX, WIDE), BF16),
            jax.ShapeDtypeStruct((1, WIDE), BF16),
            jax.ShapeDtypeStruct((NX, NY, SMALL), BF16),
            jax.ShapeDtypeStruct((2, NX, NY, 128), F32),
            jax.ShapeDtypeStruct((24, 256), F32),
        ),
        in_specs=[hbm] * len(raw),
        out_specs=(vmem,) * 6,
        scratch_shapes=[
            pltpu.VMEM((NX, 16, SMALL), F32),
            pltpu.VMEM((8, WIDE), F32),
            pltpu.SemaphoreType.DMA((len(raw),)),
        ]
        + [pltpu.VMEM(a.shape, a.dtype) for a in raw],
        compiler_params=pltpu.CompilerParams(vmem_limit_bytes=VMEM_MOST),
    )(*raw)
    halo_x = send(face_x, -1, 0)
    halo_y = send(face_y, 0, -1)
    halo_c = send(corner, -1, -1)

    wide_table, short_table = (jnp.asarray(a) for a in tab)
    near_tables = pl.pallas_call(
        local_kernel,
        out_shape=(
            jax.ShapeDtypeStruct(wide_table.shape, F32),
            jax.ShapeDtypeStruct(short_table.shape, BF16),
        ),
        in_specs=[vmem] * 2,
        out_specs=(vmem,) * 2,
        compiler_params=params,
        cost_estimate=pl.CostEstimate(
            flops=4000000, bytes_accessed=8000000, transcendentals=0
        ),
    )(wide_table, short_table)

    part, ret_x, ret_y, shares = pl.pallas_call(
        functools.partial(main_kernel, nx_dev, ny_dev),
        out_shape=(
            jax.ShapeDtypeStruct((NX, NY, BACK), F32),
            jax.ShapeDtypeStruct((NY + 1, BACK), BF16),
            jax.ShapeDtypeStruct((NX, BACK), BF16),
            jax.ShapeDtypeStruct((nx_dev * ny_dev, share_lanes), F32),
        ),
        in_specs=[vmem] * 10,
        out_specs=(vmem,) * 4,
        scratch_shapes=[
            pltpu.VMEM((ROWS, WIDE), F32),
            pltpu.VMEM((2 * ROWS, 5 * 1152), BF16),
            pltpu.VMEM((3 * PTS, 5 * 1152), F32),
            pltpu.VMEM((5, 256, 1152), F32),
            pltpu.VMEM((ROWS, COLS), F32),
            pltpu.VMEM((PTS, BACK), F32),
            pltpu.VMEM((PORTS, 64), F32),
        ],
        compiler_params=params,
        cost_estimate=pl.CostEstimate(
            flops=400000000, bytes_accessed=8000000, transcendentals=0
        ),
    )(
        par,
        tangent,
        tangent_prev,
        own,
        small,
        halo_x,
        halo_y,
        halo_c,
        *near_tables,
    )

    port_rows, port_cols = PORTS // ny_dev, 64 // nx_dev
    shares = lax.all_to_all(shares, ("gx", "gy"), 0, 0)
    back_x = send(ret_x, 1, 0)
    onward = pl.pallas_call(
        relay_kernel,
        out_shape=jax.ShapeDtypeStruct((NX + 1, BACK), BF16),
        in_specs=[vmem, vmem],
        out_specs=vmem,
        scratch_shapes=[pltpu.VMEM((8, BACK), F32)],
        compiler_params=params,
        cost_estimate=pl.CostEstimate(flops=100000, bytes_accessed=200000, transcendentals=0),
    )(back_x, ret_y)
    back_y = send(onward, 0, 1)

    tangent_next, disp_wide = pl.pallas_call(
        last_kernel,
        out_shape=(
            jax.ShapeDtypeStruct((NX, NY, COLS), BF16),
            jax.ShapeDtypeStruct((NX, NY, 128), F32),
        ),
        in_specs=[vmem] * 3,
        out_specs=(vmem, vmem),
        compiler_params=params,
        cost_estimate=pl.CostEstimate(flops=4000000, bytes_accessed=8000000, transcendentals=0),
    )(part, back_x, back_y)
    port_amp, disp_next = pl.pallas_call(
        functools.partial(final_kernel, port_rows, port_cols),
        out_shape=(
            jax.ShapeDtypeStruct((port_rows, port_cols), F32),
            jax.ShapeDtypeStruct((NX, NY, 3, NZ), BF16),
        ),
        in_specs=[vmem, vmem],
        out_specs=(vmem, vmem),
        scratch_shapes=[pltpu.VMEM((NX, NY, 3, NZ), F32)],
        compiler_params=params,
    )(shares, disp_wide)
    return (disp_next.transpose(0, 1, 3, 2), tangent_next, port_amp)


def solution(mesh):
    return jax.shard_map(
        per_device,
        mesh=mesh,
        in_specs=(
            P("gx", "gy", None, None),
            P("gx", "gy", None, None),
            P("gx", "gy", None),
            P("gx", "gy", None),
            P("gx", "gy", None),
            P("gx", "gy", None),
            P("gx", "gy", None),
            P("gx", "gy", None, None),
            P("gx", "gy", None),
            P(),
            P("gx", "gy", None),
            P("gx", "gy", None, None),
        ),
        out_specs=(P("gx", "gy", None, None), P("gx", "gy", None), P("gy", "gx")),
        check_vma=False,
    )
```

```python
import functools

import jax
import jax.numpy as jnp
import ml_dtypes
import numpy as np
from jax import lax
from jax.experimental import pallas as pl
from jax.experimental.pallas import tpu as pltpu
from jax.sharding import PartitionSpec as P

PORTS = 64
GLL_POINTS = np.array(
    [-1.0, -0.765055323929465, -0.285231516480645, 0.285231516480645, 0.765055323929465, 1.0]
)
GLL_WEIGHTS = np.array(
    [
        1.0 / 15.0,
        0.378474956297847,
        0.554858377035486,
        0.554858377035486,
        0.378474956297847,
        1.0 / 15.0,
    ]
)
STEP_SQUARED = 0.03
F32 = jnp.float32
BF16 = jnp.bfloat16

NX, NY, NZ = 5, 10, 26
COLS = 4992
SMALL = 384
WIDE = COLS + SMALL
BACK = COLS + 128
ROWS = 96
PTS = 72
VMEM_LIMIT = 24 * 1024 * 1024
VMEM_MOST = 60 * 1024 * 1024
UNROLL = 9
SHARE = 32


def derivative_table():
    identity = np.eye(6)
    differences = GLL_POINTS[:, None] - GLL_POINTS[None, :] + identity
    barycentric = 1.0 / np.prod(differences, axis=1)
    matrix = barycentric[None, :] / barycentric[:, None] / differences
    matrix = matrix * (1.0 - identity)
    matrix = matrix - identity * matrix.sum(axis=1)[:, None]
    return matrix


def halves(matrix):
    matrix = matrix.astype(np.float32)
    high = matrix.astype(ml_dtypes.bfloat16)
    low = (matrix - high.astype(np.float32)).astype(ml_dtypes.bfloat16)
    return high, low


SYM = {(0, 0): 0, (1, 1): 1, (2, 2): 2, (0, 1): 3, (0, 2): 4, (1, 2): 5}


def sym_of(c, d):
    return SYM[(min(c, d), max(c, d))]


@functools.cache
def tables():
    deriv = derivative_table()
    w = GLL_WEIGHTS
    fx = np.zeros((PTS, ROWS))
    fy = np.zeros((PTS, ROWS))
    fv = np.zeros((PTS, ROWS))
    wxy = np.zeros(PTS)
    for e in range(2):
        for px in range(6):
            for py in range(6):
                r = e * 36 + px * 6 + py
                wxy[r] = w[px] * w[py]
                fv[r, 16 * px + 5 * e + py] = 1.0
                for a in range(6):
                    fx[r, 16 * a + 5 * e + py] += deriv[px, a]
                    fy[r, 16 * px + 5 * e + a] += deriv[py, a]
    forward = np.concatenate([fx, fy, fv], axis=0)
    f_high, f_low = halves(forward)
    forward2 = np.concatenate([f_high, f_low], axis=1)
    backward = np.concatenate([(m * wxy[:, None]).T for m in (fx, fy, fv)], axis=1)
    b_high, b_low = halves(backward)
    backward2 = np.concatenate([b_high, b_low], axis=0)

    coef = np.zeros((2, 39, 128))
    for n in range(3):
        for m in range(3):
            a = np.repeat([deriv[2 * n, 2 * m], deriv[2 * n + 1, 2 * m + 1]], 64)
            b = np.repeat([deriv[2 * n, 2 * m + 1], deriv[2 * n + 1, 2 * m]], 64)
            at = np.repeat([deriv[2 * m, 2 * n], deriv[2 * m + 1, 2 * n + 1]], 64)
            bt = np.repeat([deriv[2 * m + 1, 2 * n], deriv[2 * m, 2 * n + 1]], 64)
            for q, v in enumerate((a, b, at, bt)):
                coef[0, q * 9 + n * 3 + m] = v
                coef[1, q * 9 + n * 3 + m] = np.roll(v, 64)
    for m in range(3):
        v = np.repeat([w[2 * m], w[2 * m + 1]], 64)
        coef[0, 36 + m] = v
        coef[1, 36 + m] = np.roll(v, 64)
    coef = np.repeat(coef.reshape(78, 1, 128), 8, axis=1).astype(np.float32)

    to_sym = np.zeros((3, 128, 512))
    from_sym = np.zeros((256, 384))
    merge = np.zeros((128, 128))
    for i in range(5):
        for kp in range(6):
            base = i * 36 + kp * 6
            for c in range(3):
                merge[i * 18 + c * 6 + kp, c * 32 + 5 * i + kp] = 1.0
                for d in range(3):
                    s = base + sym_of(c, d)
                    targets = [(s, 2.0 if c == d else 1.0)]
                    if c == d:
                        targets += [(256 + base + q, 1.0) for q in range(3)]
                    for column, factor in targets:
                        if d < 2:
                            to_sym[d, c * 32 + 5 * i + kp, column] += factor
                        else:
                            for k in range(6):
                                to_sym[2, c * 32 + 5 * i + k, column] += factor * deriv[kp, k]
                    if d < 2:
                        from_sym[s, d * 128 + i * 18 + c * 6 + kp] += w[kp]
                    else:
                        for k in range(6):
                            from_sym[s, 256 + i * 18 + c * 6 + k] += w[kp] * deriv[kp, k]
    spread = np.zeros((128, 128))
    for piece in range(3):
        for k in range(NZ):
            for c in range(3):
                spread[piece * 32 + k, c * 32 + k] = 1.0
    of_first = np.tile(np.arange(PTS) < 36, 3)[None, :]
    back_el = np.concatenate([backward * of_first, backward * ~of_first], axis=0)
    wide = np.zeros((1168, 512), np.float32)
    wide[0:384] = to_sym.reshape(384, 512)
    wide[384:640, 0:384] = from_sym
    wide[384:512, 384:512] = merge
    wide[640:832, 0:216] = back_el
    wide[640:952, 256:384] = coef[0:39].reshape(312, 128)
    wide[640:952, 384:512] = coef[39:78].reshape(312, 128)
    wide[952:1168, 0:192] = forward2.astype(np.float32)
    wide[952:1144, 256:472] = backward2.astype(np.float32)
    wide[512:640, 384:512] = spread
    return wide


def fdot(a, b):
    (a_high, a_low), (b_high, b_low) = split(a), split(b)
    return bdot(a_high, b_high) + (bdot(a_low, b_high) + bdot(a_high, b_low))


def bdot(a, b):
    return jnp.dot(a, b, preferred_element_type=F32)


def split(value):
    high = value.astype(BF16)
    return high, (value - high.astype(F32)).astype(BF16)


def fetch(pairs, sem):
    copies = [pltpu.make_async_copy(src, dst, sem.at[n]) for n, (src, dst) in enumerate(pairs)]
    for copy in copies:
        copy.start()
    return copies


def pack_kernel(*refs):
    sources, (x_ref, y_ref, c_ref, s_ref, own_ref, par_ref) = refs[0:11], refs[11:17]
    small, wide, sem = refs[17:20]
    here = refs[20:]
    t_ref, d_ref, m_ref, mass_ref, id_ref, dp_ref, f_ref, lam_ref, mu_ref, cell_ref, dir_ref = here
    copies = fetch(zip(sources, here, strict=True), sem)
    small[...] = jnp.zeros((NX, 16, SMALL), F32)
    own_ref[...] = jnp.zeros((2, NX, NY, 128), F32)
    for copy in copies[1:]:
        copy.wait()
    for x in range(NX):
        d = d_ref[x].astype(F32)
        m = m_ref[x].astype(F32)
        before = 2.0 * d - dp_ref[x].astype(F32)
        f = f_ref[x].astype(F32)
        for c in range(3):
            small[x, 0:NY, 32 * c : 32 * c + NZ] = d[:, c, :]
            small[x, 0:NY, 128 + 32 * c : 128 + 32 * c + NZ] = m[:, c, :]
            own_ref[0, x, :, 32 * c : 32 * c + NZ] = before[:, c, :]
            own_ref[1, x, :, 32 * c : 32 * c + NZ] = f[:, c, :]
        small[x, 0:NY, 96 : 96 + NZ] = id_ref[x].astype(F32)
        rest = mass_ref[x]
        for piece in range(3):
            part = rest.astype(BF16).astype(F32)
            small[x, 0:NY, 256 + 32 * piece : 256 + 32 * piece + NZ] = part
            rest = rest - part
        s_ref[x] = small[x, 0:NY, :].astype(BF16)
    along_z = lax.broadcasted_iota(jnp.int32, (1, 256), 1) // 36
    for q, ref in enumerate((lam_ref, mu_ref)):
        values = ref[0].astype(F32)
        for e in range(2):
            row = jnp.zeros((1, 256), F32)
            for i in range(5):
                row = jnp.where(
                    along_z == i, jnp.broadcast_to(values[e : e + 1, i : i + 1], (1, 256)), row
                )
            par_ref[2 * q + e : 2 * q + e + 1, :] = row
    dirs = jnp.concatenate([dir_ref[...], dir_ref[...]], axis=1)
    cells = cell_ref[0]
    for e in range(2):
        for i in range(5):
            same = dirs == jnp.broadcast_to(cells[e : e + 1, i : i + 1], (1, 128))
            par_ref[8 + 5 * e + i : 9 + 5 * e + i, 0:128] = jnp.where(same, 1.0, 0.0)
    copies[0].wait()
    x_ref[:, :COLS] = t_ref[0]
    x_ref[:, COLS:] = small[0, 0:NY, :].astype(BF16)
    for x in range(NX):
        wide[x : x + 1, :COLS] = t_ref[x, 0:1, :].astype(F32)
        wide[x : x + 1, COLS:] = small[x, 0:1, :]
    y_ref[...] = wide[0:NX, :].astype(BF16)
    c_ref[...] = wide[0:1, :].astype(BF16)


def local_kernel(wide_in, wide_out):
    wide_out[...] = wide_in[...]


def main_kernel(
    n_x,
    n_y,
    par_ref,
    t_ref,
    tp_ref,
    own_ref,
    s_ref,
    hx_ref,
    hy_ref,
    hc_ref,
    *rest,
):
    tab = rest[0]
    part_ref, rx_ref, ry_ref, share_ref = rest[1:5]
    (wide, uc, grad, stress, force, edge, amp) = rest[5:]

    for x in range(NX):
        wide[16 * x + 8 : 16 * x + 16, :] = jnp.zeros((8, WIDE), F32)
        wide[16 * x : 16 * x + NY, :COLS] = t_ref[x].astype(F32)
        wide[16 * x : 16 * x + NY, COLS:] = s_ref[x].astype(F32)
        wide[16 * x + NY : 16 * x + NY + 1, :] = hy_ref[x : x + 1, :].astype(F32)
    wide[88:96, :] = jnp.zeros((8, WIDE), F32)
    wide[80 : 80 + NY, :] = hx_ref[...].astype(F32)
    wide[80 + NY : 81 + NY, :] = hc_ref[...].astype(F32)

    low_rows = lax.broadcasted_iota(jnp.int32, (ROWS, 128), 1) < 64
    first_el = lax.broadcasted_iota(jnp.int32, (PTS, 128), 0) < 36
    first_el2 = lax.broadcasted_iota(jnp.int32, (PTS, 256), 0) < 36

    for i in range(5):
        odd = i % 2
        tile0 = (960 * i - 64 * odd) // 128

        def source(index, tile0=tile0):
            return wide[:, (tile0 + index) * 128 : (tile0 + index + 1) * 128]

        for m in range(3):
            t = [source(3 * m + q) for q in range(3 + odd)]
            if odd:
                by_c = (
                    jnp.where(low_rows, t[2], t[0]),
                    pltpu.roll(jnp.where(low_rows, t[1], t[2]), 64, 1),
                    jnp.where(low_rows, t[3], t[1]),
                )
            else:
                by_c = (
                    jnp.where(low_rows, t[0], t[1]),
                    pltpu.roll(jnp.where(low_rows, t[2], t[0]), 64, 1),
                    jnp.where(low_rows, t[1], t[2]),
                )
            for c in range(3):
                at = i * 1152 + (c * 3 + m) * 128
                value = by_c[c].astype(BF16)
                uc[0:ROWS, at : at + 128] = value
                uc[ROWS : 2 * ROWS, at : at + 128] = value

    fwd = tab[952:1168, 0:192].astype(BF16)
    bwd = tab[952:1144, 256:512].astype(BF16)

    small_nodes = wide[:, COLS : COLS + 128].astype(BF16)
    pg = bdot(fwd, jnp.concatenate([small_nodes, small_nodes], axis=0))
    both = fdot(pg[0:PTS], tab[0:128, :])
    both = both + fdot(pg[PTS : 2 * PTS], tab[128:256, :])
    both = both + fdot(pg[2 * PTS : 3 * PTS], tab[256:384, :])
    lam_l = jnp.where(first_el2, par_ref[0:1, :], par_ref[1:2, :])
    mu_l = jnp.where(first_el2, par_ref[2:3, :], par_ref[3:4, :])
    primal_stress = lam_l * both[:, 256:512] + mu_l * both[:, 0:256]
    unit = fdot(both[:, 0:256], tab[384:640, 0:384])
    full = fdot(primal_stress, tab[384:640, 0:384])
    terms = jnp.zeros((2 * ROWS, 256), F32)
    for d in range(3):
        pair = jnp.concatenate([a[:, d * 128 : (d + 1) * 128] for a in (unit, full)], axis=1)
        terms = terms + fdot(tab[640:832, d * PTS : (d + 1) * PTS], pair)
    unit_first, unit_second = terms[0:ROWS, 0:128], terms[ROWS : 2 * ROWS, 0:128]
    primal_force = fdot(terms[0:ROWS, 128:256] + terms[ROWS : 2 * ROWS, 128:256], tab[384:512, 384:512])

    force[...] = jnp.zeros((ROWS, COLS), F32)
    grad[...] = bdot(fwd, uc[...])
    lane = lax.broadcasted_iota(jnp.int32, (ROWS, 128), 1)
    row40 = lax.broadcasted_iota(jnp.int32, (40, 128), 0)
    half40 = lax.broadcasted_iota(jnp.int32, (40, 128), 1) // 64

    for i in range(5):
        odd = i % 2
        lam_rows, mu_rows = (
            jnp.where(
                first_el,
                *(
                    jnp.broadcast_to(par_ref[r : r + 1, 36 * i : 36 * i + 1], (PTS, 128))
                    for r in (q, q + 1)
                ),
            )
            for q in (0, 2)
        )
        edge[0:PTS, 0:128] = lam_rows
        edge[0:PTS, 128:256] = mu_rows
        pick = [par_ref[8 + 5 * e + i : 9 + 5 * e + i, 0:128] for e in range(2)]
        for c in range(3):
            for m in range(3):
                target = c * 6 + 2 * m + (1 - half40 if odd else half40)
                value = jnp.where(
                    row40 == target,
                    pick[0],
                    jnp.where(row40 == target + 18, pick[1], 0.0),
                )
                stress[i, 216:256, (c * 3 + m) * 128 : (c * 3 + m + 1) * 128] = value

        def rows_step(rc, carry, odd=odd, i=i):
            row = pl.multiple_of(rc * 8, 8)

            def tile(kind, c, m):
                at = pl.multiple_of(kind * PTS + rc * 8, 8)
                lanes = i * 1152 + (c * 3 + m) * 128
                return grad[pl.ds(at, 8), lanes : lanes + 128]

            def coef(index):
                at = 256 + 128 * odd
                return tab[640 + 8 * index : 648 + 8 * index, at : at + 128]

            def put(direction, c, m, value):
                at = pl.multiple_of(direction * PTS + rc * 8, 8)
                stress[i, pl.ds(at, 8), (c * 3 + m) * 128 : (c * 3 + m + 1) * 128] = value

            def along_z(tiles, offset):
                turned = [pltpu.roll(v, 64, 1) for v in tiles]
                return [
                    sum(
                        coef(offset + n * 3 + m) * tiles[m]
                        + coef(offset + 9 + n * 3 + m) * turned[m]
                        for m in range(3)
                    )
                    for n in range(3)
                ]

            gz = [along_z([tile(2, c, m) for m in range(3)], 0) for c in range(3)]
            lam = edge[pl.ds(row, 8), 0:128]
            mu = edge[pl.ds(row, 8), 128:256]
            z_stress = [[None] * 3 for _ in range(3)]
            for m in range(3):
                wz = coef(36 + m)
                muw = mu * wz
                g = [[tile(0, c, m) for c in range(3)], [tile(1, c, m) for c in range(3)]]
                g.append([gz[c][m] for c in range(3)])
                dil = (lam * wz) * (g[0][0] + g[1][1] + g[2][2])
                put(0, 0, m, (muw + muw) * g[0][0] + dil)
                put(1, 1, m, (muw + muw) * g[1][1] + dil)
                z_stress[2][m] = (muw + muw) * g[2][2] + dil
                value = muw * (g[0][1] + g[1][0])
                put(0, 1, m, value)
                put(1, 0, m, value)
                value = muw * (g[0][2] + g[2][0])
                put(0, 2, m, value)
                z_stress[0][m] = value
                value = muw * (g[1][2] + g[2][1])
                put(1, 2, m, value)
                z_stress[1][m] = value
            for c in range(3):
                for n, value in enumerate(along_z(z_stress[c], 18)):
                    put(2, c, n, value)
            return carry

        lax.fori_loop(0, 9, rows_step, 0, unroll=UNROLL)
        s_high = stress[i].astype(BF16)
        s_low = (stress[i, 0:216, :] - s_high[0:216].astype(F32)).astype(BF16)
        unit_here = jnp.where(
            lane < 106,
            pltpu.roll(unit_first, (88 - 18 * i) % 128, 1),
            pltpu.roll(unit_second, (106 - 18 * i) % 128, 1),
        )
        unit_high, unit_low = split(unit_here)
        unit_both = jnp.concatenate([unit_high, unit_low], axis=0)
        lane2 = lax.broadcasted_iota(jnp.int32, (2 * ROWS, 128), 1)
        inside = (lane2 >= 88) & (lane2 < 124)
        left = jnp.concatenate(
            [
                bwd[:, 0:128],
                jnp.where(inside, unit_both.astype(F32), bwd[:, 128:256].astype(F32)).astype(BF16),
            ],
            axis=1,
        )
        two = bdot(left, s_high)
        nodes = two[0:ROWS] + two[ROWS : 2 * ROWS] + bdot(bwd[0:ROWS, 0:216], s_low)

        def node_tile(c, m, nodes=nodes):
            return nodes[:, (c * 3 + m) * 128 : (c * 3 + m + 1) * 128]

        tile0 = (960 * i - 64 * odd) // 128

        def add(index, value, tile0=tile0):
            at = (tile0 + index) * 128
            force[:, at : at + 128] = force[:, at : at + 128] + value

        zero = jnp.zeros((ROWS, 128), F32)
        last_c2 = zero
        for m in range(3):
            c0, c2 = node_tile(0, m), node_tile(2, m)
            c1 = pltpu.roll(node_tile(1, m), 64, 1)
            if odd:
                add(3 * m, jnp.where(low_rows, last_c2, c0))
                add(3 * m + 1, jnp.where(low_rows, c1, c2))
                add(3 * m + 2, jnp.where(low_rows, c0, c1))
                last_c2 = c2
            else:
                add(3 * m, jnp.where(low_rows, c0, c1))
                add(3 * m + 1, jnp.where(low_rows, c2, c0))
                add(3 * m + 2, jnp.where(low_rows, c1, c2))
        if odd:
            add(9, jnp.where(low_rows, last_c2, zero))

    mass = bdot(wide[:, COLS + 256 : COLS + 384].astype(BF16), tab[512:640, 384:512].astype(BF16))
    rate = STEP_SQUARED / jnp.where(mass > 0.0, mass, 1.0)
    primal_step = -rate * primal_force
    for x in range(NX):
        part_ref[x, :, COLS:] = (
            primal_step[16 * x : 16 * x + NY, :]
            + own_ref[0, x]
            + rate[16 * x : 16 * x + NY, :] * own_ref[1, x]
        )
    rx_ref[:, COLS:] = primal_step[80 : 81 + NY, :].astype(BF16)
    for x in range(NX):
        edge[x : x + 1, COLS:BACK] = primal_step[16 * x + NY : 16 * x + NY + 1, :]

    ids = jnp.transpose(wide[:, COLS : COLS + 128])[96:128]
    ids = jnp.concatenate([ids, ids], axis=1)
    modes = jnp.transpose(wide[:, COLS + 128 : COLS + 256])
    modes = jnp.concatenate([modes, modes], axis=1)
    port = lax.broadcasted_iota(jnp.int32, (PORTS, 2 * ROWS), 0).astype(F32)
    total = jnp.zeros((128, 128), F32)
    for tile in range(39):
        at = slice(tile * 128, (tile + 1) * 128)
        two_halves = [divmod(2 * tile, 3), divmod(2 * tile + 1, 3)]
        k0, k1 = two_halves[0][0], two_halves[1][0]
        r0 = jnp.broadcast_to(rate[:, k0 : k0 + 1], (ROWS, 128))
        if k1 != k0:
            r1 = jnp.broadcast_to(rate[:, k1 : k1 + 1], (ROWS, 128))
            r0 = jnp.where(low_rows, r0, r1)
        force[:, at] = -r0 * force[:, at]
        for x in range(NX):
            rows = slice(16 * x, 16 * x + NY)
            now = force[rows, at] + 2.0 * wide[rows, at] - tp_ref[x, :, at].astype(F32)
            force[rows, at] = now
            part_ref[x, :, at] = now
        high, low = split(force[:, at])
        picked = [
            jnp.where(ids[k : k + 1, :] == port, modes[32 * c + k : 32 * c + k + 1, :], 0.0)
            for k, c in two_halves
        ]
        left = jnp.concatenate(picked, axis=0).astype(BF16)
        total = total + bdot(left, jnp.concatenate([high, low], axis=0))
    rx_ref[:, :COLS] = force[80 : 81 + NY, :].astype(BF16)
    for x in range(NX):
        edge[x : x + 1, :COLS] = force[16 * x + NY : 16 * x + NY + 1, :]
    ry_ref[...] = edge[0:NX, 0:BACK].astype(BF16)
    amp[:, 0:64] = total[0:64, 0:64] + pltpu.roll(total[64:128, :], 64, 1)[:, 0:64]
    p_rows, p_cols = PORTS // n_y, 64 // n_x
    share_ref[...] = jnp.zeros(share_ref.shape, F32)
    for q in range(p_rows):
        mine = amp[pl.ds(q, n_y, stride=p_rows), :] if p_rows > 1 else amp[...]
        for a in range(n_x):
            share_ref[a * n_y : (a + 1) * n_y, q * p_cols : (q + 1) * p_cols] = mine[
                :, a * p_cols : (a + 1) * p_cols
            ]


def relay_kernel(rx_ref, ry_ref, out_ref, rows):
    rows[0:NX, :] = ry_ref[...].astype(F32)
    rows[NX : NX + 1, :] = rx_ref[NY : NY + 1, :].astype(F32)
    out_ref[...] = rows[0 : NX + 1, :].astype(BF16)


def last_kernel(part_ref, rx_ref, ry_ref, t_ref, d_ref):
    first = lax.broadcasted_iota(jnp.int32, (NY, BACK), 0) == 0
    for x in range(NX):
        row = ry_ref[x : x + 1, :].astype(F32)
        if x == 0:
            row = row + ry_ref[NX : NX + 1, :].astype(F32)
        value = part_ref[x] + jnp.where(first, row, 0.0)
        if x == 0:
            value = value + rx_ref[0:NY, :].astype(F32)
        t_ref[x] = value[:, :COLS].astype(BF16)
        d_ref[x] = value[:, COLS:]


def final_kernel(port_rows, port_cols, share_ref, d_ref, amp_ref, out_ref, lined):
    row = jnp.sum(share_ref[...], axis=0, keepdims=True)
    for q in range(port_rows):
        amp_ref[q : q + 1, :] = row[:, q * port_cols : (q + 1) * port_cols]
    for x in range(NX):
        for c in range(3):
            lined[x, :, c, :] = d_ref[x, :, 32 * c : 32 * c + NZ]
        out_ref[x] = lined[x].astype(BF16)


def per_device(
    disp,
    disp_prev,
    tangent,
    tangent_prev,
    lame_lambda,
    lame_mu,
    node_mass,
    force,
    cell_block,
    direction_block,
    port_id,
    port_mode,
):
    tab = tables()
    share_lanes = max(SHARE, PORTS * 64 // (lax.axis_size("gx") * lax.axis_size("gy")))
    nx_dev, ny_dev = lax.axis_size("gx"), lax.axis_size("gy")
    vmem = pl.BlockSpec(memory_space=pltpu.VMEM)
    hbm = pl.BlockSpec(memory_space=pltpu.HBM)
    params = pltpu.CompilerParams(vmem_limit_bytes=VMEM_LIMIT)

    def step(shift_x, shift_y):
        route = []
        for i in range(nx_dev):
            for j in range(ny_dev):
                a, b = i + shift_x, j + shift_y
                if 0 <= a < nx_dev and 0 <= b < ny_dev:
                    route.append((i * ny_dev + j, a * ny_dev + b))
        return route

    def send(block, shift_x, shift_y):
        return lax.ppermute(block, ("gx", "gy"), step(shift_x, shift_y))

    by_comp = [a.transpose(0, 1, 3, 2) for a in (disp, port_mode, disp_prev, force)]
    raw = (tangent, by_comp[0], by_comp[1], node_mass, port_id, by_comp[2], by_comp[3])
    raw += (lame_lambda, lame_mu, cell_block, direction_block.reshape(1, 64))
    face_x, face_y, corner, small, own, par = pl.pallas_call(
        pack_kernel,
        out_shape=(
            jax.ShapeDtypeStruct((NY, WIDE), BF16),
            jax.ShapeDtypeStruct((NX, WIDE), BF16),
            jax.ShapeDtypeStruct((1, WIDE), BF16),
            jax.ShapeDtypeStruct((NX, NY, SMALL), BF16),
            jax.ShapeDtypeStruct((2, NX, NY, 128), F32),
            jax.ShapeDtypeStruct((24, 256), F32),
        ),
        in_specs=[hbm] * len(raw),
        out_specs=(vmem,) * 6,
        scratch_shapes=[
            pltpu.VMEM((NX, 16, SMALL), F32),
            pltpu.VMEM((8, WIDE), F32),
            pltpu.SemaphoreType.DMA((len(raw),)),
        ]
        + [pltpu.VMEM(a.shape, a.dtype) for a in raw],
        compiler_params=pltpu.CompilerParams(vmem_limit_bytes=VMEM_MOST),
    )(*raw)
    halo_x = send(face_x, -1, 0)
    halo_y = send(face_y, 0, -1)
    halo_c = send(corner, -1, -1)

    wide_table = jnp.asarray(tab)
    near_table = pl.pallas_call(
        local_kernel,
        out_shape=jax.ShapeDtypeStruct(wide_table.shape, F32),
        in_specs=[vmem],
        out_specs=vmem,
        compiler_params=params,
        cost_estimate=pl.CostEstimate(
            flops=4000000, bytes_accessed=8000000, transcendentals=0
        ),
    )(wide_table)

    part, ret_x, ret_y, shares = pl.pallas_call(
        functools.partial(main_kernel, nx_dev, ny_dev),
        out_shape=(
            jax.ShapeDtypeStruct((NX, NY, BACK), F32),
            jax.ShapeDtypeStruct((NY + 1, BACK), BF16),
            jax.ShapeDtypeStruct((NX, BACK), BF16),
            jax.ShapeDtypeStruct((nx_dev * ny_dev, share_lanes), F32),
        ),
        in_specs=[vmem] * 9,
        out_specs=(vmem,) * 4,
        scratch_shapes=[
            pltpu.VMEM((ROWS, WIDE), F32),
            pltpu.VMEM((2 * ROWS, 5 * 1152), BF16),
            pltpu.VMEM((3 * PTS, 5 * 1152), F32),
            pltpu.VMEM((5, 256, 1152), F32),
            pltpu.VMEM((ROWS, COLS), F32),
            pltpu.VMEM((PTS, BACK), F32),
            pltpu.VMEM((PORTS, 64), F32),
        ],
        compiler_params=params,
        cost_estimate=pl.CostEstimate(
            flops=400000000, bytes_accessed=8000000, transcendentals=0
        ),
    )(
        par,
        tangent,
        tangent_prev,
        own,
        small,
        halo_x,
        halo_y,
        halo_c,
        near_table,
    )

    port_rows, port_cols = PORTS // ny_dev, 64 // nx_dev
    shares = lax.all_to_all(shares, ("gx", "gy"), 0, 0)
    back_x = send(ret_x, 1, 0)
    onward = pl.pallas_call(
        relay_kernel,
        out_shape=jax.ShapeDtypeStruct((NX + 1, BACK), BF16),
        in_specs=[vmem, vmem],
        out_specs=vmem,
        scratch_shapes=[pltpu.VMEM((8, BACK), F32)],
        compiler_params=params,
        cost_estimate=pl.CostEstimate(flops=100000, bytes_accessed=200000, transcendentals=0),
    )(back_x, ret_y)
    back_y = send(onward, 0, 1)

    tangent_next, disp_wide = pl.pallas_call(
        last_kernel,
        out_shape=(
            jax.ShapeDtypeStruct((NX, NY, COLS), BF16),
            jax.ShapeDtypeStruct((NX, NY, 128), F32),
        ),
        in_specs=[vmem] * 3,
        out_specs=(vmem, vmem),
        compiler_params=params,
        cost_estimate=pl.CostEstimate(flops=4000000, bytes_accessed=8000000, transcendentals=0),
    )(part, back_x, back_y)
    port_amp, disp_next = pl.pallas_call(
        functools.partial(final_kernel, port_rows, port_cols),
        out_shape=(
            jax.ShapeDtypeStruct((port_rows, port_cols), F32),
            jax.ShapeDtypeStruct((NX, NY, 3, NZ), BF16),
        ),
        in_specs=[vmem, vmem],
        out_specs=(vmem, vmem),
        scratch_shapes=[pltpu.VMEM((NX, NY, 3, NZ), F32)],
        compiler_params=params,
    )(shares, disp_wide)
    return (disp_next.transpose(0, 1, 3, 2), tangent_next, port_amp)


def solution(mesh):
    return jax.shard_map(
        per_device,
        mesh=mesh,
        in_specs=(
            P("gx", "gy", None, None),
            P("gx", "gy", None, None),
            P("gx", "gy", None),
            P("gx", "gy", None),
            P("gx", "gy", None),
            P("gx", "gy", None),
            P("gx", "gy", None),
            P("gx", "gy", None, None),
            P("gx", "gy", None),
            P(),
            P("gx", "gy", None),
            P("gx", "gy", None, None),
        ),
        out_specs=(P("gx", "gy", None, None), P("gx", "gy", None), P("gy", "gx")),
        check_vma=False,
    )
```
